32 devices in a mesh: groups: 2 (over y), dp: 16 (over z, x, core).
Axes of the slice: x: 2, y: 2, z: 4, core: 2. Of those that a mesh axis runs over, the one named last changes fastest.
Arguments:
- training_output_gradients: bfloat16 [64, 256, 4096], P(('groups', 'dp')), parts along dimension 0
- training_activations: bfloat16 [64, 256, 7168], P(('groups', 'dp')), parts along dimension 0
- train_ids: int32 [64, 256], P(('groups', 'dp')), parts along dimension 0, may hold values from 0 to 128255, as said below
- seq_index: int32 [64], P(('groups', 'dp')), parts along dimension 0, may hold values from 0 to 31, each once
- left_factor: bfloat16 [4096, 1024], P('dp', 'groups'), parts along dimension 1, may hold values from -0.09375 to 0.09375
- input_side_factor: bfloat16 [7168, 1024], P('dp', 'groups'), parts along dimension 1, may hold values from -0.0625 to 0.0625
- query_ids: int32 [32, 64], P('groups'), parts along dimension 0, may hold values from 0 to 128255, as said below
Outputs:
- influence: float32 [64, 16], P(('groups', 'dp')), parts along dimension 0
The draws below stay inside these ranges and needn't reach their ends.
There are 2 independent parts, one for each index of `groups`. The reference program is written for one: setup_inputs(seed, part) draws one part's arguments, and reference() takes and returns one part's arrays. A program takes and returns all parts, laid end to end along the dimension named above; each array names one. Nothing has to cross between parts.
Inputs may be any that keep to these rules, and one draw needn't show every extreme that they name: `train_ids`: 0 marks padding and stands only at the end of a sequence; at least 128 leading tokens of every sequence are not 0. `query_ids`: 0 marks padding and stands only at the end of a completion; at least 32 leading tokens are not 0. `seq_index`: each position once.
All inputs are finite; a program needn't handle non-finite values.
Results may differ from the reference program's by a relative error of at most 0.0003.
Values may be sent and summed in bfloat16 or wider, within the bound.
No kernel may reach another device: no remote copies, remote signals or barrier semaphores. Data moves between devices by JAX's collectives and lax.ppermute only.
A program may use at most 64 MiB of HBM per device.

```python
import math
import jax
import jax.numpy as jnp
from jax import lax

D = 4096
HID = 7168
VOCAB = 128256
RANK = 32
QUERIES = 16
QLEN = 64
LEN = 256
SEQS = 32


def column_scales(key, width, low_outer, high_outer):
    key_base, key_pick, key_dimension = jax.random.split(key, 3)
    scales = jnp.exp(jax.random.uniform(key_base, (width,), jnp.float32, 0.0, math.log(10.0)))
    picked = jax.random.permutation(key_pick, width)[:4]
    outer = jnp.exp(jax.random.uniform(key_dimension, (4,), jnp.float32, math.log(low_outer), math.log(high_outer)))
    scales = scales.at[picked].set(outer)
    base_energy = 99.0 / (2.0 * math.log(10.0))
    outer_energy = (high_outer * high_outer - low_outer) / (2.0 * math.log(high_outer))
    energy = base_energy * (width - 4) / width + 4.0 * outer_energy / width
    return scales / math.sqrt(energy)


def blend(key, noise, share, spread, low_outer, high_outer):
    key_comp, key_weight, key_scale, key_column = jax.random.split(key, 4)
    rows, length, width = noise.shape
    comps = jax.random.normal(key_comp, (rows, 4, width), jnp.float32)
    weights = jax.random.normal(key_weight, (rows, length, 4), jnp.float32) * share
    scales = jnp.exp(jax.random.uniform(key_scale, (rows, length, 1), jnp.float32, 0.0, math.log(spread)))
    total = noise
    for index in range(4):
        total = total + weights[:, :, index:index + 1] * comps[:, None, index, :]
    columns = column_scales(key_column, width, low_outer, high_outer)
    return total * scales * columns[None, None, :] / math.sqrt(1.0 + 4.0 * share * share)


def draw_training_output_gradients(key, part):
    key = jax.random.fold_in(key, 11)
    key_noise, key_rest = jax.random.split(key)
    shape = (SEQS, LEN, D)
    noise = jax.random.normal(key_noise, shape, jnp.float32)
    return blend(key_rest, noise, 0.5, 2.0, 1.0, 10.0).astype(jnp.bfloat16)


def draw_training_activations(key, part):
    key = jax.random.fold_in(key, 23)
    key_noise, key_rest = jax.random.split(key)
    shape = (SEQS, LEN, HID)
    noise = jax.random.normal(key_noise, shape, jnp.float32)
    return blend(key_rest, noise, 0.5, 2.0, 1.0, 10.0).astype(jnp.bfloat16)


def padded_ids(key, rows, length):
    key_len, key_identifiers = jax.random.split(key)
    lengths = jax.random.randint(key_len, (rows,), length // 2, length + 1)
    tokens = jax.random.randint(key_identifiers, (rows, length), 1, VOCAB)
    position = jnp.arange(length, dtype=jnp.int32)
    filled = jnp.where(position[None, :] < lengths[:, None], tokens, 0).astype(jnp.int32)
    filled = filled.at[0, 0].set(VOCAB - 1)
    filled = filled.at[rows - 1, length - 1].set(0)
    return filled.astype(jnp.int32)


def draw_train_ids(key, part):
    key = jax.random.fold_in(key, 37)
    return padded_ids(key, SEQS, LEN)


def draw_query_ids(key, part):
    key = jax.random.fold_in(key, 41)
    return padded_ids(key, QUERIES, QLEN)


def levels(own_key, extent, cuts, smallest, high):
    def one(dim, shards_of):
        draws = jax.random.uniform(jax.random.fold_in(jax.random.fold_in(own_key, 6), dim), (shards_of,), jnp.float32, smallest / len(cuts), high / len(cuts))
        return jnp.repeat(jnp.exp(draws), extent[dim] // shards_of).reshape((-1,) + (1,) * (len(extent) - dim - 1))

    gain = one(*cuts[0])
    for cut in cuts[1:]:
        gain = gain * one(*cut)
    return gain


def scatter_about(own_key, shape, scale, limit, shards=(), held_as=jnp.bfloat16):
    gain = levels(own_key, shape, shards, -0.22, 0.18) if shards else 1.0
    result = jax.random.normal(own_key, shape, jnp.float32) * scale * gain
    return jnp.minimum(jnp.maximum(result, -limit), limit).astype(held_as)


def setup_inputs(seed: int = 0, part: int = 0) -> dict:
    seeds = jax.random.split(jax.random.key(seed), 8)
    part_splits = jax.random.split(jax.random.fold_in(seeds[7], part), 8)
    training_output_gradients = draw_training_output_gradients(jax.random.fold_in(jax.random.fold_in(seeds[7], part), 71), part)
    training_activations = draw_training_activations(jax.random.fold_in(jax.random.fold_in(seeds[7], part), 71), part)
    train_ids = draw_train_ids(jax.random.fold_in(jax.random.fold_in(seeds[7], part), 71), part)
    seq_index = jax.random.permutation(part_splits[3], SEQS).astype(jnp.int32)
    left_factor = scatter_about(part_splits[4], (D, QUERIES * RANK), D ** -0.5, 0.09375, ((0, 16),))
    input_side_factor = scatter_about(part_splits[5], (HID, QUERIES * RANK), HID ** -0.5, 0.0625, ((0, 16),))
    query_ids = draw_query_ids(jax.random.fold_in(jax.random.fold_in(seeds[7], part), 71), part)
    return {"training_output_gradients": training_output_gradients, "training_activations": training_activations, "train_ids": train_ids, "seq_index": seq_index, "left_factor": left_factor, "input_side_factor": input_side_factor, "query_ids": query_ids}


def one_sequence(items, left_factor, input_side_factor):
    grads, acts, ids = items
    live = (ids != 0).astype(jnp.float32)
    proj_out = jnp.dot(grads, left_factor, preferred_element_type=jnp.float32)
    proj_in = jnp.dot(acts, input_side_factor, preferred_element_type=jnp.float32)
    per_col = lax.optimization_barrier(jnp.sum(proj_out * proj_in * live[:, None], axis=0))
    raw = lax.optimization_barrier(jnp.sum(per_col.reshape(QUERIES, RANK), axis=1))
    grads32 = grads.astype(jnp.float32)
    acts32 = acts.astype(jnp.float32)
    output_covariance = jnp.einsum('ld,md->lm', grads32, grads32)
    input_covariance = jnp.einsum('ld,md->lm', acts32, acts32)
    grad_sq = jnp.sum(live[:, None] * live[None, :] * output_covariance * input_covariance)
    return (raw, grad_sq)

def reference(training_output_gradients, training_activations, train_ids, seq_index, left_factor, input_side_factor, query_ids):
    raw, grad_sq = lax.map(lambda items: one_sequence(items, left_factor, input_side_factor), (training_output_gradients, training_activations, train_ids))
    count = lax.optimization_barrier(jnp.sum((query_ids != 0).astype(jnp.float32), axis=1))
    factor = QLEN * math.sqrt(D * HID / RANK)
    score = raw * factor / (count[None, :] * jnp.sqrt(grad_sq + 1e-06)[:, None])
    influence = jnp.zeros((SEQS, QUERIES), jnp.float32).at[seq_index].set(score)
    return influence
```

```python
import functools
import math

import jax
import jax.numpy as jnp
from jax import lax
from jax.experimental import pallas as pl
from jax.experimental.pallas import tpu as pltpu
from jax.sharding import PartitionSpec as P

AXIS = "dp"
MIB = 1 << 20


def ring_order(chips):
    return list(range(0, chips, 2)) + list(range(chips - 1, 0, -2))


def xor_pairs(devices, mask):
    return [(i, i ^ mask) for i in range(devices)]


def ring_pairs(order, shift):
    chips = len(order)
    return [
        (order[k] * 2 + core, order[(k + shift) % chips] * 2 + core)
        for k in range(chips)
        for core in range(2)
    ]


def send(x, pairs):
    return lax.ppermute(x, AXIS, pairs)


def in_order(*values):
    return lax.optimization_barrier(values)


def device_index():
    return lax.axis_index(AXIS)


def chip_on_ring(chips, chip, shift):
    place = jnp.where(chip % 2 == 0, chip // 2, chips - 1 - chip // 2)
    place = (place + shift + chips) % chips
    return jnp.where(place < chips // 2, 2 * place, 2 * (chips - 1 - place) + 1)


SMEM = pl.BlockSpec(memory_space=pltpu.SMEM)
VMEM = pl.BlockSpec(memory_space=pltpu.VMEM)
ANY = pl.BlockSpec(memory_space=pl.ANY)
FLOAT = jnp.float32


def params(limit=60):
    return pltpu.CompilerParams(vmem_limit_bytes=limit * MIB)


def small_cost():
    return pl.CostEstimate(flops=1, bytes_accessed=1, transcendentals=0)


def dot(a, b):
    return jnp.dot(a, b, preferred_element_type=FLOAT)


def dot_rows(a, b, precision=None):
    return lax.dot_general(
        a, b, (((1,), (1,)), ((), ())), precision=precision, preferred_element_type=FLOAT
    )


def exact_dot(a, b):
    return jnp.dot(a, b, precision=lax.Precision.HIGHEST, preferred_element_type=FLOAT)


class Rows:
    def __init__(self, chip, side, first, own, partner):
        self.chip, self.side, self.first = chip, side, first
        self.own, self.partner = own, partner

    def copies(self, per_device, own, partner, stacks, sems):
        core = device_index() % 2
        count = own.shape[0]
        result = []
        for j, (piece, place) in enumerate(((own, core), (partner, 1 - core))):
            base = place * per_device[self.side] + self.first
            target = stacks[self.side].at[self.chip, pl.ds(pl.multiple_of(base, 16), count), :]
            result.append(pltpu.make_async_copy(piece, target, sems.at[j]))
        return result


def project_kernel(per_device, shifts, chips, rows, fresh, *refs):
    grads, acts, refs = refs[0], refs[1], refs[2:]
    pieces, refs = refs[: 2 * len(rows)], refs[2 * len(rows) :]
    if not fresh:
        before, refs = refs[0], refs[1:]
    sums, left, right, lefts, rights, total, row_sems, block_sems, sum_sems = refs
    chip = device_index() // 2
    row_copies = [
        r.copies(per_device, pieces[2 * i], pieces[2 * i + 1], (lefts, rights), row_sems.at[i])
        for i, r in enumerate(rows)
    ]
    loads = []
    for k, shift in enumerate(shifts):
        there = chip_on_ring(chips, chip, shift)
        for j, (features, block) in enumerate(((grads, left), (acts, right))):
            width = block.shape[2]
            columns = pl.ds(pl.multiple_of(there * width, 128), width)
            loads.append(
                pltpu.make_async_copy(features.at[:, columns], block.at[k], block_sems.at[k, j])
            )
    old = [] if fresh else [
        pltpu.make_async_copy(before.at[j], total.at[j], sum_sems.at[0, j]) for j in range(2)
    ]
    new = [pltpu.make_async_copy(total.at[j], sums.at[j], sum_sems.at[1, j]) for j in range(2)]
    for j in range(2):
        for load in loads[j::2]:
            load.start()
        for r, copies in zip(rows, row_copies):
            if r.side == j:
                for copy in copies:
                    copy.start()
        if not fresh:
            old[j].start()
    for j, (block, stack) in enumerate(((left, lefts), (right, rights))):
        for load in loads[j::2]:
            load.wait()
        for r, copies in zip(rows, row_copies):
            if r.side == j:
                for copy in copies:
                    copy.wait()
        terms = [dot(block[k], stack[k]) for k in range(len(shifts))]
        if not fresh:
            old[j].wait()
            terms.append(total[j])
        total[j] = sum(terms)
        new[j].start()
    for copy in new:
        copy.wait()


def project(chips, shifts, grads, acts, per_device, rows, sums):
    count, tokens = len(shifts), grads.shape[0]
    columns = rows[0].own.shape[1]
    widths = [2 * n for n in per_device]
    sum_shape = (2, tokens, columns)
    before = [] if sums is None else [sums]
    pieces = [piece for r in rows for piece in (r.own, r.partner)]
    return pl.pallas_call(
        functools.partial(project_kernel, per_device, shifts, chips, rows, not before),
        in_specs=[ANY] * (2 + len(pieces) + len(before)),
        out_specs=ANY,
        out_shape=jax.ShapeDtypeStruct(sum_shape, FLOAT),
        scratch_shapes=[pltpu.VMEM((count, tokens, w), grads.dtype) for w in widths]
        + [pltpu.VMEM((count, w, columns), grads.dtype) for w in widths]
        + [
            pltpu.VMEM(sum_shape, FLOAT),
            pltpu.SemaphoreType.DMA((len(rows), 2)),
            pltpu.SemaphoreType.DMA((count, 2)),
            pltpu.SemaphoreType.DMA((2, 2)),
        ],
        compiler_params=params(),
        cost_estimate=small_cost(),
    )(grads, acts, *pieces, *before)


def fetch_kernel(chips, shift, grads, acts, left, right, left_held, right_held, sems):
    there = chip_on_ring(chips, device_index() // 2, shift)
    loads, stores = [], []
    for j, (features, held, block) in enumerate(
        ((grads, left_held, left), (acts, right_held, right))
    ):
        width = block.shape[1]
        columns = pl.ds(pl.multiple_of(there * width, 128), width)
        loads.append(pltpu.make_async_copy(features.at[:, columns], held, sems.at[j, 0]))
        stores.append(pltpu.make_async_copy(held, block, sems.at[j, 1]))
    for load in loads:
        load.start()
    for load, store in zip(loads, stores):
        load.wait()
        store.start()
    for store in stores:
        store.wait()


def fetch(chips, shift, grads, acts):
    shapes = [(x.shape[0], x.shape[1] // chips) for x in (grads, acts)]
    return pl.pallas_call(
        functools.partial(fetch_kernel, chips, shift),
        in_specs=[ANY, ANY],
        out_specs=[ANY, ANY],
        out_shape=[jax.ShapeDtypeStruct(s, grads.dtype) for s in shapes],
        scratch_shapes=[pltpu.VMEM(s, grads.dtype) for s in shapes]
        + [pltpu.SemaphoreType.DMA((2, 2))],
        compiler_params=params(),
        cost_estimate=small_cost(),
    )(grads, acts)


def finish_kernel(per_device, rows, rank, factor, *refs):
    pieces, refs = refs[: 2 * len(rows)], refs[2 * len(rows) :]
    left, right, sums, info, query_ids, dense, lefts, rights, sems = refs
    row_copies = [
        copy
        for i, r in enumerate(rows)
        for copy in r.copies(
            per_device, pieces[2 * i], pieces[2 * i + 1], (lefts, rights), sems.at[i]
        )
    ]
    for copy in row_copies:
        copy.start()
    columns = lefts.shape[2]
    queries = dense.shape[1]
    length = info.shape[2] - 128
    sequences = info.shape[0]
    column = lax.broadcasted_iota(jnp.int32, (columns, queries), 0)
    query = lax.broadcasted_iota(jnp.int32, (columns, queries), 1)
    member = (column // rank == query).astype(FLOAT)
    slot = lax.broadcasted_iota(jnp.int32, dense.shape, 0).astype(FLOAT)
    asked = (query_ids[...] != 0).astype(FLOAT)
    count = dot_rows(jnp.ones((8, asked.shape[1]), FLOAT), asked, lax.Precision.HIGHEST)
    placed = jnp.zeros(dense.shape, FLOAT)
    for copy in row_copies:
        copy.wait()
    for s in range(sequences):
        here = slice(s * length, (s + 1) * length)
        product = (sums[0, here, :] + dot(left[here, :], lefts[0])) * (
            sums[1, here, :] + dot(right[here, :], rights[0])
        )
        raw = exact_dot(exact_dot(info[s, :, 0:length], product), member)
        norm = jnp.sqrt(info[s, :, length : length + 1] + 1e-06)
        score = raw * factor / (count * norm)
        place = info[s, 0:1, length + 1 : length + 2]
        placed = placed + jnp.where(slot == place, score[0:1, :], 0.0)
    dense[...] = placed


def finish(per_device, rows, blocks, sums, info, query_ids, slots, rank, factor):
    columns = rows[0].own.shape[1]
    pieces = [piece for r in rows for piece in (r.own, r.partner)]
    return pl.pallas_call(
        functools.partial(finish_kernel, per_device, rows, rank, factor),
        in_specs=[ANY] * len(pieces) + [VMEM] * 5,
        out_specs=VMEM,
        out_shape=jax.ShapeDtypeStruct((slots, query_ids.shape[0]), FLOAT),
        scratch_shapes=[pltpu.VMEM((1, 2 * n, columns), pieces[0].dtype) for n in per_device]
        + [pltpu.SemaphoreType.DMA((len(rows), 2))],
        compiler_params=params(20),
        cost_estimate=small_cost(),
    )(*pieces, *blocks, sums, info, query_ids)


def info_kernel(steps, sequence, seq_index, grads, acts, ids, info, out_cov, in_cov):
    step = pl.program_id(0)

    @pl.when(step == 0)
    def _():
        out_cov[...] = dot_rows(grads[0], grads[0])

    for k in range(1, steps):

        @pl.when(step == k)
        def _(k=k):
            term = dot_rows(acts[0], acts[0])
            if k > 1:
                term = in_cov[...] + term
            if k < steps - 1:
                in_cov[...] = term
            else:
                length = out_cov.shape[0]
                live = jnp.broadcast_to((ids[0] != 0).astype(FLOAT), (8, length))
                rows = exact_dot(live, term * out_cov[...]) * live
                norm = jnp.sum(rows, axis=1, keepdims=True)
                lane = lax.broadcasted_iota(jnp.int32, (8, 128), 1)
                place = seq_index[sequence].astype(FLOAT)
                info[0, :, 0:length] = live
                info[0, :, length:] = jnp.where(lane == 0, norm, jnp.where(lane == 1, place, 0.0))


def sequence_info(sequence, seq_index, train_ids, grads, acts):
    length, width = grads.shape[1:]
    hidden = acts.shape[2]
    parts = 2 if hidden % 256 == 0 else 1
    steps = 1 + parts
    return pl.pallas_call(
        functools.partial(info_kernel, steps, sequence),
        grid=(steps,),
        in_specs=[
            SMEM,
            pl.BlockSpec((1, length, width), lambda k: (sequence, 0, 0)),
            pl.BlockSpec(
                (1, length, hidden // parts), lambda k: (sequence, 0, jnp.maximum(k - 1, 0))
            ),
            pl.BlockSpec((1, 1, length), lambda k: (sequence, 0, 0)),
        ],
        out_specs=pl.BlockSpec((1, 8, length + 128), lambda k: (0, 0, 0)),
        out_shape=jax.ShapeDtypeStruct((1, 8, length + 128), FLOAT),
        scratch_shapes=[pltpu.VMEM((length, length), FLOAT)] * 2,
        compiler_params=params(),
        cost_estimate=small_cost(),
    )(seq_index, grads, acts, train_ids[:, None, :])


def squared_norms(live, grads, acts):
    def covariance(x):
        return jnp.einsum("hcp,hqp->hcq", x, x, preferred_element_type=jnp.float32)

    return jnp.sum(
        live[:, :, None] * live[:, None, :] * covariance(grads) * covariance(acts), axis=(1, 2)
    )


def to_owners(dense, seq_count):
    devices = lax.axis_size(AXIS)
    if devices & (devices - 1):
        return lax.psum_scatter(dense, AXIS, scatter_dimension=0, tiled=True)
    mask = 1
    while mask < devices:
        dense = dense + send(dense, xor_pairs(devices, mask))
        mask *= 2
    return lax.dynamic_slice_in_dim(dense, lax.axis_index(AXIS) * seq_count, seq_count, axis=0)


def by_gathers(
    training_output_gradients, training_activations, train_ids, seq_index,
    left_factor, input_side_factor, query_ids,
):
    seq_count, length, width = training_output_gradients.shape
    hidden = training_activations.shape[2]
    columns = left_factor.shape[1]
    queries = query_ids.shape[0]
    rank = columns // queries
    grads = training_output_gradients.reshape(seq_count * length, width)
    acts = training_activations.reshape(seq_count * length, hidden)
    proj_out = dot(grads, lax.all_gather(left_factor, AXIS, axis=0, tiled=True))
    proj_in = dot(acts, lax.all_gather(input_side_factor, AXIS, axis=0, tiled=True))
    live = (train_ids != 0).astype(jnp.float32)
    product = (proj_out * proj_in).reshape(seq_count, length, columns) * live[:, :, None]
    raw = jnp.sum(jnp.sum(product, axis=1).reshape(seq_count, queries, rank), axis=2)
    grad_sq = squared_norms(live, training_output_gradients, training_activations)
    count = jnp.sum((query_ids != 0).astype(jnp.float32), axis=1)
    factor = query_ids.shape[1] * math.sqrt(width * hidden / rank)
    score = raw * factor / (count[None, :] * jnp.sqrt(grad_sq + 1e-06)[:, None])
    slots = jnp.arange(seq_count * lax.axis_size(AXIS), dtype=jnp.int32)
    dense = jnp.sum(
        jnp.where(seq_index[:, None, None] == slots[None, :, None], score[:, None, :], 0.0), axis=0
    )
    return to_owners(dense, seq_count)


def by_ring(
    training_output_gradients, training_activations, train_ids, seq_index,
    left_factor, input_side_factor, query_ids,
):
    seq_count, length, width = training_output_gradients.shape
    hidden = training_activations.shape[2]
    columns = left_factor.shape[1]
    queries = query_ids.shape[0]
    rank = columns // queries
    devices = lax.axis_size(AXIS)
    chips = devices // 2
    hops = chips // 2
    swap = xor_pairs(devices, 1)
    order = ring_order(chips)
    forward, backward = ring_pairs(order, 1), ring_pairs(order, -1)
    grads = training_output_gradients.reshape(seq_count * length, width)
    acts = training_activations.reshape(seq_count * length, hidden)
    per_device = (left_factor.shape[0], input_side_factor.shape[0])

    def with_partner(chip, side, first, piece):
        return Rows(chip, side, first, piece, send(piece, swap))

    lefts = [send(left_factor, forward), send(left_factor, backward)]
    rights = [send(input_side_factor, forward), send(input_side_factor, backward)]
    near = [with_partner(0, 0, 0, left_factor), with_partner(0, 1, 0, input_side_factor)]
    infos = [
        sequence_info(s, seq_index, train_ids, training_output_gradients, training_activations)
        for s in range(seq_count)
    ]
    sums = project(chips, [0], grads, acts, per_device, near, None)
    cut = (per_device[1] - per_device[0]) // 2 // 16 * 16
    for hop in range(1, hops):
        *lefts, sums = in_order(*lefts, sums)
        if hop <= len(infos):
            lefts[0], infos[hop - 1] = in_order(lefts[0], infos[hop - 1])
        behind = [with_partner(0, 0, 0, lefts[0])]
        ahead = [with_partner(1, 0, 0, lefts[1])]
        left_f, left_b = lefts
        lefts = [send(left_f, forward)]
        if hop + 1 < hops:
            lefts.append(send(left_b, backward))
        right_f, right_b = in_order(*rights)
        behind.append(with_partner(0, 1, 0, right_f))
        ahead.append(with_partner(1, 1, 0, right_b))
        if hop + 1 < hops:
            rights = [send(right_f, forward), send(right_b, backward)]
        else:
            rights = [send(right_f[:cut], forward), send(right_b[cut:], backward)]
        rows = [*behind, *ahead]
        sums = project(chips, [-hop, hop], grads, acts, per_device, rows, sums)
    rows = [
        with_partner(0, 0, 0, lefts[0]),
        with_partner(0, 1, 0, rights[0]),
        with_partner(0, 1, cut, rights[1]),
    ]
    blocks = fetch(chips, hops, grads, acts)
    info = jnp.concatenate(infos, axis=0)
    factor = query_ids.shape[1] * math.sqrt(width * hidden / rank)
    dense = finish(
        per_device, rows, blocks, sums, info, query_ids, seq_count * devices, rank, factor
    )
    return to_owners(dense, seq_count)


def on_device(*args):
    left_rows, right_rows = args[4].shape[0], args[5].shape[0]
    devices = lax.axis_size(AXIS)
    fits = (
        devices % 4 == 0
        and left_rows % 64 == 0
        and right_rows % 64 == 0
        and args[4].shape[1] % 256 == 0
        and args[6].shape[0] % 2 == 0
        and args[0].shape[1] % 128 == 0
        and (2 * left_rows) % 128 == 0
        and (2 * right_rows) % 128 == 0
    )
    return by_ring(*args) if fits else by_gathers(*args)


def solution(mesh):
    in_specs = (
        P(("groups", "dp"), None, None),
        P(("groups", "dp"), None, None),
        P(("groups", "dp"), None),
        P(("groups", "dp")),
        P("dp", "groups"),
        P("dp", "groups"),
        P("groups", None),
    )
    out_specs = P(("groups", "dp"), None)
    return jax.shard_map(
        on_device, mesh=mesh, in_specs=in_specs, out_specs=out_specs, check_vma=False
    )
```

```python
import functools
import math

import jax
import jax.numpy as jnp
from jax import lax
from jax.experimental import pallas as pl
from jax.experimental.pallas import tpu as pltpu
from jax.sharding import PartitionSpec as P

AXIS = "dp"
MIB = 1 << 20
ROWS = 256


def ring_order(chips):
    return list(range(0, chips, 2)) + list(range(chips - 1, 0, -2))


def xor_pairs(devices, mask):
    return [(i, i ^ mask) for i in range(devices)]


def ring_pairs(order, shift):
    chips = len(order)
    return [
        (order[k] * 2 + core, order[(k + shift) % chips] * 2 + core)
        for k in range(chips)
        for core in range(2)
    ]


def send(x, pairs):
    return lax.ppermute(x, AXIS, pairs)


def in_order(*values):
    return lax.optimization_barrier(values)


def device_index():
    return lax.axis_index(AXIS)


def chip_on_ring(chips, chip, shift):
    place = jnp.where(chip % 2 == 0, chip // 2, chips - 1 - chip // 2)
    place = (place + shift + chips) % chips
    return jnp.where(place < chips // 2, 2 * place, 2 * (chips - 1 - place) + 1)


SMEM = pl.BlockSpec(memory_space=pltpu.SMEM)
VMEM = pl.BlockSpec(memory_space=pltpu.VMEM)
ANY = pl.BlockSpec(memory_space=pl.ANY)
FLOAT = jnp.float32


def params(limit=60):
    return pltpu.CompilerParams(vmem_limit_bytes=limit * MIB)


def small_cost():
    return pl.CostEstimate(flops=1, bytes_accessed=1, transcendentals=0)


def dot(a, b):
    return jnp.dot(a, b, preferred_element_type=FLOAT)


def dot_rows(a, b, precision=None):
    return lax.dot_general(
        a, b, (((1,), (1,)), ((), ())), precision=precision, preferred_element_type=FLOAT
    )


def exact_dot(a, b):
    return jnp.dot(a, b, precision=lax.Precision.HIGHEST, preferred_element_type=FLOAT)


def split_kernel(left, right, mine, other):
    core = device_index() % 2
    low = left.shape[0]
    half = mine.shape[1]

    def put(target, first):
        target[0:low, :] = left[:, first : first + half]
        target[low:, :] = right[:, first : first + half]

    @pl.when(core == 0)
    def _():
        put(mine, 0)
        put(other, half)

    @pl.when(core != 0)
    def _():
        put(mine, half)
        put(other, 0)


def split_columns(left, right):
    rows, half = left.shape[0] + right.shape[0], left.shape[1] // 2
    return pl.pallas_call(
        split_kernel,
        in_specs=[VMEM, VMEM],
        out_specs=[VMEM, VMEM],
        out_shape=[jax.ShapeDtypeStruct((rows, half), left.dtype)] * 2,
        compiler_params=params(8),
        cost_estimate=small_cost(),
    )(left, right)


def merge_kernel(low, mine, came, piece):
    core = device_index() % 2
    high = mine.shape[0] - low

    def put(first, second):
        piece[0:low, :] = first[0:low, :]
        piece[low : 2 * low, :] = second[0:low, :]
        piece[2 * low : 2 * low + high, :] = first[low:, :]
        piece[2 * low + high :, :] = second[low:, :]

    @pl.when(core == 0)
    def _():
        put(mine, came)

    @pl.when(core != 0)
    def _():
        put(came, mine)


def merge_rows(low, mine, came):
    rows, half = mine.shape
    return pl.pallas_call(
        functools.partial(merge_kernel, low),
        in_specs=[VMEM, VMEM],
        out_specs=VMEM,
        out_shape=jax.ShapeDtypeStruct((2 * rows, half), mine.dtype),
        compiler_params=params(8),
        cost_estimate=small_cost(),
    )(mine, came)


def block_of(chips, shift, features, rows=slice(None)):
    width = features.shape[1] // chips
    there = chip_on_ring(chips, device_index() // 2, shift)
    return features[rows, pl.ds(pl.multiple_of(there * width, 128), width)]


def project_kernel(shifts, chips, fresh, *refs):
    features, refs = refs[:2], refs[2:]
    pieces, refs = refs[: len(shifts)], refs[len(shifts) :]
    before, sums = (None, refs[0]) if fresh else refs
    split = features[0].shape[1] // chips

    @pl.loop(0, features[0].shape[0] // ROWS)
    def _(i):
        rows = pl.ds(pl.multiple_of(i * ROWS, ROWS), ROWS)
        for j, part in enumerate((slice(0, split), slice(split, None))):
            terms = [] if fresh else [before[j, rows, :]]
            for shift, piece in zip(shifts, pieces):
                terms.append(dot(block_of(chips, shift, features[j], rows), piece[part, :]))
            sums[j, rows, :] = sum(terms)


def project(chips, shifts, features, pieces, sums):
    tokens, columns = features[0].shape[0], pieces[0].shape[1]
    before = [] if sums is None else [sums]
    return pl.pallas_call(
        functools.partial(project_kernel, shifts, chips, not before),
        in_specs=[VMEM] * (2 + len(pieces) + len(before)),
        out_specs=VMEM,
        out_shape=jax.ShapeDtypeStruct((2, tokens, columns), FLOAT),
        input_output_aliases={2 + len(pieces): 0} if before else {},
        compiler_params=params(8),
        cost_estimate=small_cost(),
    )(*features, *pieces, *before)


def finish_kernel(
    shift, chips, rank, seq_index, seq_index_other, grads, acts, grads_other, acts_other,
    upper, lower, sums, sums_other, norms, dense, per_column,
):
    columns = upper.shape[1]
    queries = dense.shape[1] - 1
    sequences = seq_index.shape[0]
    length = grads.shape[0] // sequences
    middle, split = upper.shape[0], grads.shape[1] // chips
    core = device_index() % 2
    column = lax.broadcasted_iota(jnp.int32, (columns, queries + 1), 0)
    query = lax.broadcasted_iota(jnp.int32, (columns, queries + 1), 1)
    member = (column // rank + core * (columns // rank) == query).astype(FLOAT)
    for side, (left, right, total) in enumerate(
        ((grads, acts, sums), (grads_other, acts_other, sums_other))
    ):
        lefts, rights = block_of(chips, shift, left), block_of(chips, shift, right)
        rest = middle - split
        product = (total[0] + dot(lefts, upper[0:split, :])) * (
            total[1]
            + dot(rights[:, 0:rest], upper[split:, :])
            + dot(rights[:, rest:], lower[...])
        )
        for s in range(sequences):
            n = side * sequences + s
            per_column[n : n + 1, :] = jnp.sum(
                product[s * length : (s + 1) * length, :], axis=0, keepdims=True
            )
    raw = exact_dot(per_column[...], member)
    slot = lax.broadcasted_iota(jnp.int32, dense.shape, 0)
    lane = lax.broadcasted_iota(jnp.int32, (1, queries + 1), 1)
    placed = jnp.zeros(dense.shape, FLOAT)
    for side, places in enumerate((seq_index, seq_index_other)):
        for s in range(sequences):
            n = side * sequences + s
            row = raw[n : n + 1, :]
            if side == 0:
                row = row + jnp.where(lane == queries, norms[s, 0:1, 0:1], 0.0)
            placed = placed + jnp.where(slot == places[s], row, 0.0)
    dense[...] = placed


def finish(chips, shift, places, features, pieces, sums, norms, slots, queries, rank):
    columns = pieces[0].shape[1]
    return pl.pallas_call(
        functools.partial(finish_kernel, shift, chips, rank),
        in_specs=[SMEM] * 2 + [VMEM] * 9,
        out_specs=VMEM,
        out_shape=jax.ShapeDtypeStruct((slots, queries + 1), FLOAT),
        scratch_shapes=[pltpu.VMEM((2 * places[0].shape[0], columns), FLOAT)],
        compiler_params=params(12),
        cost_estimate=small_cost(),
    )(*places, *features, *pieces, *sums, norms)


def norms_kernel(sequences, grads, acts, norms):
    length = grads.shape[0] // sequences
    for s in range(sequences):
        rows = slice(s * length, (s + 1) * length)
        value = dot_rows(grads[rows, :], grads[rows, :]) * dot_rows(acts[rows, :], acts[rows, :])
        norms[s] = jnp.broadcast_to(jnp.sum(value, keepdims=True), norms.shape[1:])


def squared_norms_of(sequences, grads, acts):
    return pl.pallas_call(
        functools.partial(norms_kernel, sequences),
        in_specs=[VMEM, VMEM],
        out_specs=VMEM,
        out_shape=jax.ShapeDtypeStruct((sequences, 8, 128), FLOAT),
        compiler_params=params(8),
        cost_estimate=small_cost(),
    )(grads, acts)


def squared_norms(live, grads, acts):
    def covariance(x):
        return jnp.einsum("hcp,hqp->hcq", x, x, preferred_element_type=jnp.float32)

    return jnp.sum(
        live[:, :, None] * live[:, None, :] * covariance(grads) * covariance(acts), axis=(1, 2)
    )


def to_owners(dense, seq_count, mask=1):
    devices = lax.axis_size(AXIS)
    if devices & (devices - 1):
        return lax.psum_scatter(dense, AXIS, scatter_dimension=0, tiled=True)
    while mask < devices:
        masks = [mask] if mask < 4 or 2 * mask >= devices else [3 * mask, 2 * mask, mask]
        dense = sum([send(dense, xor_pairs(devices, m)) for m in masks], dense)
        mask *= len(masks) + 1
    return lax.dynamic_slice_in_dim(dense, lax.axis_index(AXIS) * seq_count, seq_count, axis=0)


def by_gathers(
    training_output_gradients, training_activations, train_ids, seq_index,
    left_factor, input_side_factor, query_ids,
):
    seq_count, length, width = training_output_gradients.shape
    hidden = training_activations.shape[2]
    columns = left_factor.shape[1]
    queries = query_ids.shape[0]
    rank = columns // queries
    grads = training_output_gradients.reshape(seq_count * length, width)
    acts = training_activations.reshape(seq_count * length, hidden)
    proj_out = dot(grads, lax.all_gather(left_factor, AXIS, axis=0, tiled=True))
    proj_in = dot(acts, lax.all_gather(input_side_factor, AXIS, axis=0, tiled=True))
    live = (train_ids != 0).astype(jnp.float32)
    product = (proj_out * proj_in).reshape(seq_count, length, columns) * live[:, :, None]
    raw = jnp.sum(jnp.sum(product, axis=1).reshape(seq_count, queries, rank), axis=2)
    grad_sq = squared_norms(live, training_output_gradients, training_activations)
    count = jnp.sum((query_ids != 0).astype(jnp.float32), axis=1)
    factor = query_ids.shape[1] * math.sqrt(width * hidden / rank)
    score = raw * factor / (count[None, :] * jnp.sqrt(grad_sq + 1e-06)[:, None])
    slots = jnp.arange(seq_count * lax.axis_size(AXIS), dtype=jnp.int32)
    dense = jnp.sum(
        jnp.where(seq_index[:, None, None] == slots[None, :, None], score[:, None, :], 0.0), axis=0
    )
    return to_owners(dense, seq_count)


def by_ring(
    training_output_gradients, training_activations, train_ids, seq_index,
    left_factor, input_side_factor, query_ids,
):
    seq_count, length, width = training_output_gradients.shape
    hidden = training_activations.shape[2]
    columns = left_factor.shape[1]
    queries = query_ids.shape[0]
    rank = columns // queries
    devices = lax.axis_size(AXIS)
    chips = devices // 2
    hops = chips // 2
    swap = xor_pairs(devices, 1)
    order = ring_order(chips)
    forward, backward = ring_pairs(order, 1), ring_pairs(order, -1)
    grads = training_output_gradients.reshape(seq_count * length, width)
    acts = training_activations.reshape(seq_count * length, hidden)
    low = left_factor.shape[0]

    mine, other = split_columns(left_factor, input_side_factor)
    came = send(other, swap)
    piece = merge_rows(low, mine, came)
    moving = [send(piece, forward), send(piece, backward)]
    grads_sent, _ = in_order(grads, came)
    acts = jnp.where((train_ids != 0).reshape(-1, 1), acts, jnp.zeros_like(acts))
    features = [grads, acts]
    features_other = [send(grads_sent, swap)]
    places = [seq_index, send(seq_index, swap)]
    norms = squared_norms_of(seq_count, grads, acts)
    shifts, pieces = [0], [piece]
    sums = sums_other = None
    middle = piece.shape[0] // 2
    for hop in range(1, hops):
        *new, norms, acts_sent, places, sums = in_order(*moving, norms, acts, places, sums)
        if hop + 1 < hops:
            moving = [send(new[0], forward), send(new[1], backward)]
        else:
            moving = [send(new[0][:middle], forward), send(new[1][middle:], backward)]
        shifts, pieces = shifts + [-hop, hop], pieces + new
        if hop == 1:
            features_other.append(send(acts_sent, swap))
            sums = project(chips, shifts, features, pieces, None)
        else:
            sums = project(chips, [-hop, hop], features, new, sums)
    sums_other = project(chips, shifts, features_other, pieces, None)
    *last, sums, sums_other = in_order(*moving, sums, sums_other)
    dense = finish(
        chips, hops, places, [*features, *features_other], last, [sums, sums_other], norms,
        seq_count * devices, queries, rank,
    )
    dense = dense + send(dense, swap)
    count = jnp.sum((query_ids != 0).astype(jnp.float32), axis=1)
    factor = query_ids.shape[1] * math.sqrt(width * hidden / rank)
    score = dense[:, :queries] * (factor / count)[None, :] / jnp.sqrt(dense[:, queries:] + 1e-06)
    return to_owners(score, seq_count, 2)


def on_device(*args):
    left_rows, right_rows = args[4].shape[0], args[5].shape[0]
    devices = lax.axis_size(AXIS)
    fits = (
        devices % 4 == 0
        and left_rows % 64 == 0
        and right_rows % 64 == 0
        and args[4].shape[1] % 256 == 0
        and args[6].shape[0] % 2 == 0
        and args[0].shape[1] % 128 == 0
        and (2 * left_rows) % 128 == 0
        and (2 * right_rows) % 128 == 0
    )
    return by_ring(*args) if fits else by_gathers(*args)


def solution(mesh):
    in_specs = (
        P(("groups", "dp"), None, None),
        P(("groups", "dp"), None, None),
        P(("groups", "dp"), None),
        P(("groups", "dp")),
        P("dp", "groups"),
        P("dp", "groups"),
        P("groups", None),
    )
    out_specs = P(("groups", "dp"), None)
    return jax.shard_map(
        on_device, mesh=mesh, in_specs=in_specs, out_specs=out_specs, check_vma=False
    )
```

```python
import functools
import math

import jax
import jax.numpy as jnp
from jax import lax
from jax.experimental import pallas as pl
from jax.experimental.pallas import tpu as pltpu
from jax.sharding import PartitionSpec as P

AXIS = "dp"
MIB = 1 << 20
ROWS = 256


def ring_order(chips):
    return list(range(0, chips, 2)) + list(range(chips - 1, 0, -2))


def xor_pairs(devices, mask):
    return [(i, i ^ mask) for i in range(devices)]


def ring_pairs(order, shift):
    chips = len(order)
    return [
        (order[k] * 2 + core, order[(k + shift) % chips] * 2 + core)
        for k in range(chips)
        for core in range(2)
    ]


def send(x, pairs):
    return lax.ppermute(x, AXIS, pairs)


def in_order(*values):
    return lax.optimization_barrier(values)


def device_index():
    return lax.axis_index(AXIS)


def chip_on_ring(chips, chip, shift):
    place = jnp.where(chip % 2 == 0, chip // 2, chips - 1 - chip // 2)
    place = (place + shift + chips) % chips
    return jnp.where(place < chips // 2, 2 * place, 2 * (chips - 1 - place) + 1)


SMEM = pl.BlockSpec(memory_space=pltpu.SMEM)
VMEM = pl.BlockSpec(memory_space=pltpu.VMEM)
ANY = pl.BlockSpec(memory_space=pl.ANY)
FLOAT = jnp.float32


def params(limit=60):
    return pltpu.CompilerParams(vmem_limit_bytes=limit * MIB)


def small_cost():
    return pl.CostEstimate(flops=1, bytes_accessed=1, transcendentals=0)


def dot(a, b):
    return jnp.dot(a, b, preferred_element_type=FLOAT)


def dot_rows(a, b, precision=None):
    return lax.dot_general(
        a, b, (((1,), (1,)), ((), ())), precision=precision, preferred_element_type=FLOAT
    )


def exact_dot(a, b):
    return jnp.dot(a, b, precision=lax.Precision.HIGHEST, preferred_element_type=FLOAT)


def split_kernel(left, right, mine, other):
    core = device_index() % 2
    low = left.shape[0]
    half = mine.shape[1]

    def put(target, first):
        target[0:low, :] = left[:, first : first + half]
        target[low:, :] = right[:, first : first + half]

    @pl.when(core == 0)
    def _():
        put(mine, 0)
        put(other, half)

    @pl.when(core != 0)
    def _():
        put(mine, half)
        put(other, 0)


def split_columns(left, right):
    rows, half = left.shape[0] + right.shape[0], left.shape[1] // 2
    return pl.pallas_call(
        split_kernel,
        in_specs=[VMEM, VMEM],
        out_specs=[VMEM, VMEM],
        out_shape=[jax.ShapeDtypeStruct((rows, half), left.dtype)] * 2,
        compiler_params=params(8),
        cost_estimate=small_cost(),
    )(left, right)


def merge_kernel(low, mine, came, upper, lower):
    core = device_index() % 2
    middle, total = upper.shape[0], upper.shape[0] + lower.shape[0]
    high = mine.shape[0] - low

    def put(first, second):
        parts = ((first, 0, low), (second, 0, low), (first, low, high), (second, low, high))
        at = 0
        for source, begin, count in parts:
            for target, start, stop in ((upper, 0, middle), (lower, middle, total)):
                lo, hi = max(at, start), min(at + count, stop)
                if lo < hi:
                    target[lo - start : hi - start, :] = source[begin + lo - at : begin + hi - at, :]
            at += count

    @pl.when(core == 0)
    def _():
        put(mine, came)

    @pl.when(core != 0)
    def _():
        put(came, mine)


def merge_rows(low, mine, came):
    return pl.pallas_call(
        functools.partial(merge_kernel, low),
        in_specs=[VMEM, VMEM],
        out_specs=[VMEM, VMEM],
        out_shape=[jax.ShapeDtypeStruct(mine.shape, mine.dtype)] * 2,
        compiler_params=params(8),
        cost_estimate=small_cost(),
    )(mine, came)


def block_of(chips, shift, features, rows=slice(None)):
    width = features.shape[1] // chips
    there = chip_on_ring(chips, device_index() // 2, shift)
    return features[rows, pl.ds(pl.multiple_of(there * width, 128), width)]


LEFT, RIGHT = 0, 1


class Job:
    def __init__(self, side, features, shifts, pieces, before=None):
        self.side, self.features, self.shifts, self.before = side, features, shifts, before
        self.pieces = pieces if side == RIGHT else pieces[::2]

    def operands(self):
        return [self.features, *self.pieces, *([] if self.before is None else [self.before])]


def project_kernel(jobs, split, chips, keep, *refs):
    rights = sum(len(job.shifts) for job in jobs if job.side == RIGHT)
    stacks, refs = (refs[-1], refs[:-1]) if rights else (None, refs)
    count = sum(len(job.operands()) for job in jobs)
    refs, outs = list(refs[:count]), list(refs[count:])
    work, used = [], 0
    for job in jobs:
        taken = [refs.pop(0) for _ in job.operands()]
        features, before = taken[0], None if job.before is None else taken.pop()
        factors = taken[1:]
        if job.side == RIGHT:
            for k in range(len(job.shifts)):
                upper, lower = factors[2 * k : 2 * k + 2]
                rest = upper.shape[0] - split
                stacks[used + k, 0:rest, :] = upper[split:, :]
                stacks[used + k, rest:, :] = lower[...]
            factors = [stacks.at[used + k] for k in range(len(job.shifts))]
            used += len(job.shifts)
        else:
            factors = [upper.at[0:split, :] for upper in factors]
        work.append((job, features, factors, before, outs.pop(0)))

    @pl.loop(0, work[0][1].shape[0] // ROWS)
    def _(i):
        rows = pl.ds(pl.multiple_of(i * ROWS, ROWS), ROWS)
        for job, features, factors, before, total in work:
            terms = [] if before is None else [before[rows, :]]
            for shift, factor in zip(job.shifts, factors):
                terms.append(dot(block_of(chips, shift, features, rows), factor[...]))
            total[rows, :] = sum(terms)
        if keep:
            outs[0][rows, :] = work[0][1][rows, :]


def project(chips, split, jobs, keep=False):
    first = jobs[0]
    tokens, columns = first.features.shape[0], first.pieces[0].shape[1]
    rights = [job for job in jobs if job.side == RIGHT]
    shapes = [jax.ShapeDtypeStruct((tokens, columns), FLOAT) for _ in jobs]
    if keep:
        shapes.append(jax.ShapeDtypeStruct(first.features.shape, first.features.dtype))
    aliases, place = {}, 0
    for k, job in enumerate(jobs):
        place += len(job.operands())
        if job.before is not None:
            aliases[place - 1] = k
    scratch = []
    if rights:
        total = sum(len(job.shifts) for job in rights)
        width = rights[0].features.shape[1] // chips
        scratch = [pltpu.VMEM((total, width, columns), first.features.dtype)]
    return pl.pallas_call(
        functools.partial(project_kernel, jobs, split, chips, keep),
        in_specs=[VMEM] * place,
        out_specs=[VMEM] * len(shapes),
        out_shape=shapes,
        scratch_shapes=scratch,
        input_output_aliases=aliases,
        compiler_params=params(14),
        cost_estimate=small_cost(),
    )(*[x for job in jobs for x in job.operands()])


def finish_kernel(
    shift, chips, rank, seq_index, seq_index_other, grads, acts, grads_other, acts_other,
    *refs,
):
    pieces, refs = refs[:-8], refs[-8:]
    sums, sums_other = refs[0:2], refs[2:4]
    norms, dense, per_column, stack = refs[4:]
    columns = stack.shape[1]
    queries = dense.shape[1] - 1
    sequences = seq_index.shape[0]
    length = grads.shape[0] // sequences
    split = grads.shape[1] // chips
    core = device_index() % 2
    column = lax.broadcasted_iota(jnp.int32, (columns, queries + 1), 0)
    query = lax.broadcasted_iota(jnp.int32, (columns, queries + 1), 1)
    member = (column // rank + core * (columns // rank) == query).astype(FLOAT)
    first = 0
    for piece in pieces:
        stack[first : first + piece.shape[0], :] = piece[...]
        first += piece.shape[0]
    sides = (
        (block_of(chips, shift, grads), block_of(chips, shift, acts), sums),
        (block_of(chips, shift, grads_other), block_of(chips, shift, acts_other), sums_other),
    )
    for side, (lefts, rights, total) in enumerate(sides):
        product = (total[0][...] + dot(lefts, stack[0:split, :])) * (
            total[1][...] + dot(rights, stack[split:, :])
        )
        for s in range(sequences):
            n = side * sequences + s
            per_column[n : n + 1, :] = jnp.sum(
                product[s * length : (s + 1) * length, :], axis=0, keepdims=True
            )
    raw = exact_dot(per_column[...], member)
    slot = lax.broadcasted_iota(jnp.int32, dense.shape, 0)
    lane = lax.broadcasted_iota(jnp.int32, (1, queries + 1), 1)
    placed = jnp.zeros(dense.shape, FLOAT)
    for side, places in enumerate((seq_index, seq_index_other)):
        for s in range(sequences):
            n = side * sequences + s
            row = raw[n : n + 1, :]
            if side == 0:
                row = row + jnp.where(lane == queries, norms[s, 0:1, 0:1], 0.0)
            placed = placed + jnp.where(slot == places[s], row, 0.0)
    dense[...] = placed


def finish(chips, shift, places, features, pieces, sums, norms, slots, queries, rank):
    columns = pieces[0].shape[1]
    return pl.pallas_call(
        functools.partial(finish_kernel, shift, chips, rank),
        in_specs=[SMEM] * 2 + [VMEM] * (9 + len(pieces)),
        out_specs=VMEM,
        out_shape=jax.ShapeDtypeStruct((slots, queries + 1), FLOAT),
        scratch_shapes=[
            pltpu.VMEM((2 * places[0].shape[0], columns), FLOAT),
            pltpu.VMEM((sum(p.shape[0] for p in pieces), columns), pieces[0].dtype),
        ],
        compiler_params=params(12),
        cost_estimate=small_cost(),
    )(*places, *features, *pieces, *sums, norms)


def norms_kernel(sequences, grads, acts, norms):
    length = grads.shape[0] // sequences
    for s in range(sequences):
        rows = slice(s * length, (s + 1) * length)
        value = dot_rows(grads[rows, :], grads[rows, :]) * dot_rows(acts[rows, :], acts[rows, :])
        norms[s] = jnp.broadcast_to(jnp.sum(value, keepdims=True), norms.shape[1:])


def squared_norms_of(sequences, grads, acts):
    return pl.pallas_call(
        functools.partial(norms_kernel, sequences),
        in_specs=[VMEM, VMEM],
        out_specs=VMEM,
        out_shape=jax.ShapeDtypeStruct((sequences, 8, 128), FLOAT),
        compiler_params=params(8),
        cost_estimate=small_cost(),
    )(grads, acts)


def squared_norms(live, grads, acts):
    def covariance(x):
        return jnp.einsum("hcp,hqp->hcq", x, x, preferred_element_type=jnp.float32)

    return jnp.sum(
        live[:, :, None] * live[:, None, :] * covariance(grads) * covariance(acts), axis=(1, 2)
    )


def to_owners(dense, seq_count, mask=1):
    devices = lax.axis_size(AXIS)
    if devices & (devices - 1):
        return lax.psum_scatter(dense, AXIS, scatter_dimension=0, tiled=True)
    while mask < devices:
        masks = [mask] if mask < 4 or 2 * mask >= devices else [3 * mask, 2 * mask, mask]
        dense = sum([send(dense, xor_pairs(devices, m)) for m in masks], dense)
        mask *= len(masks) + 1
    return lax.dynamic_slice_in_dim(dense, lax.axis_index(AXIS) * seq_count, seq_count, axis=0)


def by_gathers(
    training_output_gradients, training_activations, train_ids, seq_index,
    left_factor, input_side_factor, query_ids,
):
    seq_count, length, width = training_output_gradients.shape
    hidden = training_activations.shape[2]
    columns = left_factor.shape[1]
    queries = query_ids.shape[0]
    rank = columns // queries
    grads = training_output_gradients.reshape(seq_count * length, width)
    acts = training_activations.reshape(seq_count * length, hidden)
    proj_out = dot(grads, lax.all_gather(left_factor, AXIS, axis=0, tiled=True))
    proj_in = dot(acts, lax.all_gather(input_side_factor, AXIS, axis=0, tiled=True))
    live = (train_ids != 0).astype(jnp.float32)
    product = (proj_out * proj_in).reshape(seq_count, length, columns) * live[:, :, None]
    raw = jnp.sum(jnp.sum(product, axis=1).reshape(seq_count, queries, rank), axis=2)
    grad_sq = squared_norms(live, training_output_gradients, training_activations)
    count = jnp.sum((query_ids != 0).astype(jnp.float32), axis=1)
    factor = query_ids.shape[1] * math.sqrt(width * hidden / rank)
    score = raw * factor / (count[None, :] * jnp.sqrt(grad_sq + 1e-06)[:, None])
    slots = jnp.arange(seq_count * lax.axis_size(AXIS), dtype=jnp.int32)
    dense = jnp.sum(
        jnp.where(seq_index[:, None, None] == slots[None, :, None], score[:, None, :], 0.0), axis=0
    )
    return to_owners(dense, seq_count)


def by_ring(
    training_output_gradients, training_activations, train_ids, seq_index,
    left_factor, input_side_factor, query_ids,
):
    seq_count, length, width = training_output_gradients.shape
    hidden = training_activations.shape[2]
    columns = left_factor.shape[1]
    queries = query_ids.shape[0]
    rank = columns // queries
    devices = lax.axis_size(AXIS)
    chips = devices // 2
    hops = chips // 2
    swap = xor_pairs(devices, 1)
    order = ring_order(chips)
    forward, backward = ring_pairs(order, 1), ring_pairs(order, -1)
    grads = training_output_gradients.reshape(seq_count * length, width)
    acts = training_activations.reshape(seq_count * length, hidden)
    low = left_factor.shape[0]

    mine, other = split_columns(left_factor, input_side_factor)
    came = send(other, swap)
    pieces = list(merge_rows(low, mine, came))
    moving = [[send(x, forward), send(x, backward)] for x in pieces]
    grads_sent, _ = in_order(grads, came)
    acts = jnp.where((train_ids != 0).reshape(-1, 1), acts, jnp.zeros_like(acts))
    features = [grads, acts]
    grads_other = send(grads_sent, swap)
    places = [seq_index, send(seq_index, swap)]
    norms = squared_norms_of(seq_count, grads, acts)
    middle = pieces[0].shape[0] // 2
    split = width // chips
    shifts = [0]
    own = [None, None]
    other = [None, None]
    for hop in range(1, hops):
        if hop == 1:
            moving, norms, places, acts_sent, grads_other = in_order(
                moving, norms, places, acts, grads_other
            )
            acts_other = send(acts_sent, swap)
            new = moving
        else:
            upper, own, other[LEFT] = in_order(moving[0], own, other[LEFT])
            lower = moving[1]
            if hop + 1 == hops:
                (other[RIGHT],) = project(
                    chips, split, [Job(RIGHT, acts_other, shifts, pieces)]
                )
                *lower, other[RIGHT] = in_order(*lower, other[RIGHT])
            new = [upper, lower]
        arrived = [new[0][0], new[1][0], new[0][1], new[1][1]]
        if hop + 1 == hops:
            new = [[x[0][:middle], x[1][middle:]] for x in new]
        moving = [[send(x[0], forward), send(x[1], backward)] for x in new]
        step = [-hop, hop]
        shifts, pieces = shifts + step, pieces + arrived
        if hop == 1:
            jobs = [Job(LEFT, grads_other, shifts, pieces)]
            jobs += [Job(j, features[j], shifts, pieces) for j in (LEFT, RIGHT)]
            other[LEFT], *own, grads_other = project(chips, split, jobs, True)
        else:
            jobs = [Job(LEFT, grads_other, step, arrived, other[LEFT])]
            jobs += [Job(j, features[j], step, arrived, own[j]) for j in (LEFT, RIGHT)]
            if hop + 1 == hops:
                jobs.append(Job(RIGHT, acts_other, step, arrived, other[RIGHT]))
            if hop + 1 < hops:
                other[LEFT], *own = project(chips, split, jobs)
            else:
                own = project(chips, split, jobs[1:3])
                other = project(chips, split, jobs[:1] + jobs[3:])
    upper, lower = moving
    upper, own, other = in_order(upper, own, other)
    last = [*upper, *lower]
    dense = finish(
        chips, hops, places, [*features, grads_other, acts_other], last, [*own, *other], norms,
        seq_count * devices, queries, rank,
    )
    dense = dense + send(dense, swap)
    count = jnp.sum((query_ids != 0).astype(jnp.float32), axis=1)
    factor = query_ids.shape[1] * math.sqrt(width * hidden / rank)
    score = dense[:, :queries] * (factor / count)[None, :] / jnp.sqrt(dense[:, queries:] + 1e-06)
    return to_owners(score, seq_count, 2)


def on_device(*args):
    left_rows, right_rows = args[4].shape[0], args[5].shape[0]
    devices = lax.axis_size(AXIS)
    fits = (
        devices % 4 == 0
        and left_rows % 64 == 0
        and right_rows % 64 == 0
        and args[4].shape[1] % 256 == 0
        and args[6].shape[0] % 2 == 0
        and args[0].shape[1] % 128 == 0
        and (2 * left_rows) % 128 == 0
        and (2 * right_rows) % 128 == 0
    )
    return by_ring(*args) if fits else by_gathers(*args)


def solution(mesh):
    in_specs = (
        P(("groups", "dp"), None, None),
        P(("groups", "dp"), None, None),
        P(("groups", "dp"), None),
        P(("groups", "dp")),
        P("dp", "groups"),
        P("dp", "groups"),
        P("groups", None),
    )
    out_specs = P(("groups", "dp"), None)
    return jax.shard_map(
        on_device, mesh=mesh, in_specs=in_specs, out_specs=out_specs, check_vma=False
    )
```

```python
import functools
import math

import jax
import jax.numpy as jnp
from jax import lax
from jax.experimental import pallas as pl
from jax.experimental.pallas import tpu as pltpu
from jax.sharding import PartitionSpec as P

AXIS = "dp"
MIB = 1 << 20
ROWS = 256


def ring_order(chips):
    return list(range(0, chips, 2)) + list(range(chips - 1, 0, -2))


def xor_pairs(devices, mask):
    return [(i, i ^ mask) for i in range(devices)]


def ring_pairs(order, shift):
    chips = len(order)
    return [
        (order[k] * 2 + core, order[(k + shift) % chips] * 2 + core)
        for k in range(chips)
        for core in range(2)
    ]


def send(x, pairs):
    return lax.ppermute(x, AXIS, pairs)


def in_order(*values):
    return lax.optimization_barrier(values)


def device_index():
    return lax.axis_index(AXIS)


def chip_on_ring(chips, chip, shift):
    place = jnp.where(chip % 2 == 0, chip // 2, chips - 1 - chip // 2)
    place = (place + shift + chips) % chips
    return jnp.where(place < chips // 2, 2 * place, 2 * (chips - 1 - place) + 1)


SMEM = pl.BlockSpec(memory_space=pltpu.SMEM)
VMEM = pl.BlockSpec(memory_space=pltpu.VMEM)
ANY = pl.BlockSpec(memory_space=pl.ANY)
FLOAT = jnp.float32


def params(limit=60):
    return pltpu.CompilerParams(vmem_limit_bytes=limit * MIB)


def small_cost():
    return pl.CostEstimate(flops=1, bytes_accessed=1, transcendentals=0)


def dot(a, b):
    return jnp.dot(a, b, preferred_element_type=FLOAT)


def dot_rows(a, b, precision=None):
    return lax.dot_general(
        a, b, (((1,), (1,)), ((), ())), precision=precision, preferred_element_type=FLOAT
    )


def exact_dot(a, b):
    return jnp.dot(a, b, precision=lax.Precision.HIGHEST, preferred_element_type=FLOAT)


def split_kernel(left, right, mine, other):
    core = device_index() % 2
    low = left.shape[0]
    half = mine.shape[1]

    def put(target, first):
        target[0:low, :] = left[:, first : first + half]
        target[low:, :] = right[:, first : first + half]

    @pl.when(core == 0)
    def _():
        put(mine, 0)
        put(other, half)

    @pl.when(core != 0)
    def _():
        put(mine, half)
        put(other, 0)


def split_columns(left, right):
    rows, half = left.shape[0] + right.shape[0], left.shape[1] // 2
    return pl.pallas_call(
        split_kernel,
        in_specs=[VMEM, VMEM],
        out_specs=[VMEM, VMEM],
        out_shape=[jax.ShapeDtypeStruct((rows, half), left.dtype)] * 2,
        compiler_params=params(8),
        cost_estimate=small_cost(),
    )(left, right)


def merge_kernel(low, mine, came, upper, lower):
    core = device_index() % 2
    middle, total = upper.shape[0], upper.shape[0] + lower.shape[0]
    high = mine.shape[0] - low

    def put(first, second):
        parts = ((first, 0, low), (second, 0, low), (first, low, high), (second, low, high))
        at = 0
        for source, begin, count in parts:
            for target, start, stop in ((upper, 0, middle), (lower, middle, total)):
                lo, hi = max(at, start), min(at + count, stop)
                if lo < hi:
                    target[lo - start : hi - start, :] = source[begin + lo - at : begin + hi - at, :]
            at += count

    @pl.when(core == 0)
    def _():
        put(mine, came)

    @pl.when(core != 0)
    def _():
        put(came, mine)


def merge_rows(low, mine, came):
    return pl.pallas_call(
        functools.partial(merge_kernel, low),
        in_specs=[VMEM, VMEM],
        out_specs=[VMEM, VMEM],
        out_shape=[jax.ShapeDtypeStruct(mine.shape, mine.dtype)] * 2,
        compiler_params=params(8),
        cost_estimate=small_cost(),
    )(mine, came)


def block_of(chips, shift, features, rows=slice(None)):
    width = features.shape[1] // chips
    there = chip_on_ring(chips, device_index() // 2, shift)
    return features[rows, pl.ds(pl.multiple_of(there * width, 128), width)]


LEFT, RIGHT = 0, 1


class Job:
    def __init__(self, side, features, shifts, pieces, before=None):
        self.side, self.features, self.shifts, self.before = side, features, shifts, before
        self.pieces = pieces if side == RIGHT else pieces[::2]

    def operands(self):
        return [self.features, *self.pieces, *([] if self.before is None else [self.before])]


def project_kernel(jobs, split, chips, keep, *refs):
    rights = sum(len(job.shifts) for job in jobs if job.side == RIGHT)
    stacks, refs = (refs[-1], refs[:-1]) if rights else (None, refs)
    count = sum(len(job.operands()) for job in jobs)
    refs, outs = list(refs[:count]), list(refs[count:])
    work, used = [], 0
    for job in jobs:
        taken = [refs.pop(0) for _ in job.operands()]
        features, before = taken[0], None if job.before is None else taken.pop()
        factors = taken[1:]
        if job.side == RIGHT:
            for k in range(len(job.shifts)):
                upper, lower = factors[2 * k : 2 * k + 2]
                rest = upper.shape[0] - split
                stacks[used + k, 0:rest, :] = upper[split:, :]
                stacks[used + k, rest:, :] = lower[...]
            factors = [stacks.at[used + k] for k in range(len(job.shifts))]
            used += len(job.shifts)
        else:
            factors = [upper.at[0:split, :] for upper in factors]
        work.append((job, features, factors, before, outs.pop(0)))

    @pl.loop(0, work[0][1].shape[0] // ROWS)
    def _(i):
        rows = pl.ds(pl.multiple_of(i * ROWS, ROWS), ROWS)
        for job, features, factors, before, total in work:
            terms = [] if before is None else [before[rows, :]]
            for shift, factor in zip(job.shifts, factors):
                terms.append(dot(block_of(chips, shift, features, rows), factor[...]))
            total[rows, :] = sum(terms)
        if keep:
            outs[0][rows, :] = work[0][1][rows, :]


def project(chips, split, jobs, keep=False):
    first = jobs[0]
    tokens, columns = first.features.shape[0], first.pieces[0].shape[1]
    rights = [job for job in jobs if job.side == RIGHT]
    shapes = [jax.ShapeDtypeStruct((tokens, columns), FLOAT) for _ in jobs]
    if keep:
        shapes.append(jax.ShapeDtypeStruct(first.features.shape, first.features.dtype))
    aliases, place = {}, 0
    for k, job in enumerate(jobs):
        place += len(job.operands())
        if job.before is not None:
            aliases[place - 1] = k
    scratch = []
    if rights:
        total = sum(len(job.shifts) for job in rights)
        width = rights[0].features.shape[1] // chips
        scratch = [pltpu.VMEM((total, width, columns), first.features.dtype)]
    return pl.pallas_call(
        functools.partial(project_kernel, jobs, split, chips, keep),
        in_specs=[VMEM] * place,
        out_specs=[VMEM] * len(shapes),
        out_shape=shapes,
        scratch_shapes=scratch,
        input_output_aliases=aliases,
        compiler_params=params(14),
        cost_estimate=small_cost(),
    )(*[x for job in jobs for x in job.operands()])


def finish_kernel(
    shift, chips, rank, queries, seq_index, seq_index_other, grads, acts, grads_other,
    acts_other, *refs,
):
    pieces, refs = refs[:-8], refs[-8:]
    sums, sums_other = refs[0:2], refs[2:4]
    norms, dense, per_column, stack = refs[4:]
    columns = stack.shape[1]
    sequences = seq_index.shape[0]
    length = grads.shape[0] // sequences
    lanes = dense.shape[2] // sequences
    split = grads.shape[1] // chips
    core = device_index() % 2
    column = lax.broadcasted_iota(jnp.int32, (columns, dense.shape[2]), 0)
    query = lax.broadcasted_iota(jnp.int32, (columns, dense.shape[2]), 1) % lanes
    member = (column // rank + core * (columns // rank) == query).astype(FLOAT)
    first = 0
    for piece in pieces:
        stack[first : first + piece.shape[0], :] = piece[...]
        first += piece.shape[0]
    sides = (
        (block_of(chips, shift, grads), block_of(chips, shift, acts), sums),
        (block_of(chips, shift, grads_other), block_of(chips, shift, acts_other), sums_other),
    )
    for side, (lefts, rights, total) in enumerate(sides):
        product = (total[0][...] + dot(lefts, stack[0:split, :])) * (
            total[1][...] + dot(rights, stack[split:, :])
        )
        for s in range(sequences):
            n = side * sequences + s
            per_column[n : n + 1, :] = jnp.sum(
                product[s * length : (s + 1) * length, :], axis=0, keepdims=True
            )
    raw = exact_dot(per_column[...], member)
    lane = lax.broadcasted_iota(jnp.int32, dense.shape, 2)
    slot = lax.broadcasted_iota(jnp.int32, dense.shape, 0) * sequences + lane // lanes
    last = lane[0] % lanes == queries
    placed = jnp.zeros(dense.shape, FLOAT)
    for side, places in enumerate((seq_index, seq_index_other)):
        for s in range(sequences):
            n = side * sequences + s
            row = raw[n : n + 1, :]
            if side == 0:
                row = row + jnp.where(last, norms[s, 0:1, 0:1], 0.0)
            placed = placed + jnp.where(slot == places[s], row[None], 0.0)
    dense[...] = placed


def settle_kernel(factor, parts, query_ids, influence):
    sequences, queries = influence.shape
    lanes = parts.shape[2] // sequences
    total = jnp.sum(parts[...], axis=0)
    asked = (query_ids[...] != 0).astype(FLOAT)
    count = dot_rows(jnp.ones((8, asked.shape[1]), FLOAT), asked, lax.Precision.HIGHEST)[0:1, :]
    for s in range(sequences):
        at = s * lanes
        norm = jnp.sqrt(total[:, at + queries : at + queries + 1] + 1e-06)
        influence[s : s + 1, :] = total[:, at : at + queries] * factor / (count * norm)


def settle(parts, query_ids, sequences, factor):
    return pl.pallas_call(
        functools.partial(settle_kernel, factor),
        in_specs=[VMEM, VMEM],
        out_specs=VMEM,
        out_shape=jax.ShapeDtypeStruct((sequences, query_ids.shape[0]), FLOAT),
        compiler_params=params(4),
        cost_estimate=small_cost(),
    )(parts, query_ids)


def finish(chips, shift, places, features, pieces, sums, norms, queries, rank):
    columns = pieces[0].shape[1]
    lanes = -(-places[0].shape[0] * (queries + 1) // 128) * 128
    return pl.pallas_call(
        functools.partial(finish_kernel, shift, chips, rank, queries),
        in_specs=[SMEM] * 2 + [VMEM] * (9 + len(pieces)),
        out_specs=VMEM,
        out_shape=jax.ShapeDtypeStruct((2 * chips, 1, lanes), FLOAT),
        scratch_shapes=[
            pltpu.VMEM((2 * places[0].shape[0], columns), FLOAT),
            pltpu.VMEM((sum(p.shape[0] for p in pieces), columns), pieces[0].dtype),
        ],
        compiler_params=params(12),
        cost_estimate=small_cost(),
    )(*places, *features, *pieces, *sums, norms)


def norms_kernel(sequences, grads, acts, norms):
    length = grads.shape[0] // sequences
    for s in range(sequences):
        rows = slice(s * length, (s + 1) * length)
        value = dot_rows(grads[rows, :], grads[rows, :]) * dot_rows(acts[rows, :], acts[rows, :])
        norms[s] = jnp.broadcast_to(jnp.sum(value, keepdims=True), norms.shape[1:])


def squared_norms_of(sequences, grads, acts):
    return pl.pallas_call(
        functools.partial(norms_kernel, sequences),
        in_specs=[VMEM, VMEM],
        out_specs=VMEM,
        out_shape=jax.ShapeDtypeStruct((sequences, 8, 128), FLOAT),
        compiler_params=params(8),
        cost_estimate=small_cost(),
    )(grads, acts)


def squared_norms(live, grads, acts):
    def covariance(x):
        return jnp.einsum("hcp,hqp->hcq", x, x, preferred_element_type=jnp.float32)

    return jnp.sum(
        live[:, :, None] * live[:, None, :] * covariance(grads) * covariance(acts), axis=(1, 2)
    )


def to_owners(dense, seq_count, mask=1):
    devices = lax.axis_size(AXIS)
    if devices & (devices - 1):
        return lax.psum_scatter(dense, AXIS, scatter_dimension=0, tiled=True)
    while mask < devices:
        masks = [mask] if mask < 4 or 2 * mask >= devices else [3 * mask, 2 * mask, mask]
        dense = sum([send(dense, xor_pairs(devices, m)) for m in masks], dense)
        mask *= len(masks) + 1
    return lax.dynamic_slice_in_dim(dense, lax.axis_index(AXIS) * seq_count, seq_count, axis=0)


def by_gathers(
    training_output_gradients, training_activations, train_ids, seq_index,
    left_factor, input_side_factor, query_ids,
):
    seq_count, length, width = training_output_gradients.shape
    hidden = training_activations.shape[2]
    columns = left_factor.shape[1]
    queries = query_ids.shape[0]
    rank = columns // queries
    grads = training_output_gradients.reshape(seq_count * length, width)
    acts = training_activations.reshape(seq_count * length, hidden)
    proj_out = dot(grads, lax.all_gather(left_factor, AXIS, axis=0, tiled=True))
    proj_in = dot(acts, lax.all_gather(input_side_factor, AXIS, axis=0, tiled=True))
    live = (train_ids != 0).astype(jnp.float32)
    product = (proj_out * proj_in).reshape(seq_count, length, columns) * live[:, :, None]
    raw = jnp.sum(jnp.sum(product, axis=1).reshape(seq_count, queries, rank), axis=2)
    grad_sq = squared_norms(live, training_output_gradients, training_activations)
    count = jnp.sum((query_ids != 0).astype(jnp.float32), axis=1)
    factor = query_ids.shape[1] * math.sqrt(width * hidden / rank)
    score = raw * factor / (count[None, :] * jnp.sqrt(grad_sq + 1e-06)[:, None])
    slots = jnp.arange(seq_count * lax.axis_size(AXIS), dtype=jnp.int32)
    dense = jnp.sum(
        jnp.where(seq_index[:, None, None] == slots[None, :, None], score[:, None, :], 0.0), axis=0
    )
    return to_owners(dense, seq_count)


def by_ring(
    training_output_gradients, training_activations, train_ids, seq_index,
    left_factor, input_side_factor, query_ids,
):
    seq_count, length, width = training_output_gradients.shape
    hidden = training_activations.shape[2]
    columns = left_factor.shape[1]
    queries = query_ids.shape[0]
    rank = columns // queries
    devices = lax.axis_size(AXIS)
    chips = devices // 2
    hops = chips // 2
    swap = xor_pairs(devices, 1)
    order = ring_order(chips)
    forward, backward = ring_pairs(order, 1), ring_pairs(order, -1)
    grads = training_output_gradients.reshape(seq_count * length, width)
    acts = training_activations.reshape(seq_count * length, hidden)
    low = left_factor.shape[0]

    mine, other = split_columns(left_factor, input_side_factor)
    came = send(other, swap)
    pieces = list(merge_rows(low, mine, came))
    pieces, grads_sent, train_ids, seq_index = in_order(pieces, grads, train_ids, seq_index)
    moving = [[send(x, forward), send(x, backward)] for x in pieces]
    acts = jnp.where((train_ids != 0).reshape(-1, 1), acts, jnp.zeros_like(acts))
    features = [grads, acts]
    grads_other = send(grads_sent, swap)
    places = [seq_index, send(seq_index, swap)]
    norms = squared_norms_of(seq_count, grads, acts)
    middle = pieces[0].shape[0] // 2
    split = width // chips
    shifts = [0]
    own = [None, None]
    other = [None, None]
    for hop in range(1, hops):
        if hop == 1:
            moving, norms, places, acts_sent, grads_other = in_order(
                moving, norms, places, acts, grads_other
            )
            acts_other = send(acts_sent, swap)
            new = moving
        else:
            upper, own, other[LEFT] = in_order(moving[0], own, other[LEFT])
            lower = moving[1]
            if hop + 1 == hops:
                (other[RIGHT],) = project(
                    chips, split, [Job(RIGHT, acts_other, shifts, pieces)]
                )
                *lower, other[RIGHT] = in_order(*lower, other[RIGHT])
            new = [upper, lower]
        arrived = [new[0][0], new[1][0], new[0][1], new[1][1]]
        if hop + 1 == hops:
            new = [[x[0][:middle], x[1][middle:]] for x in new]
        moving = [[send(x[0], forward), send(x[1], backward)] for x in new]
        step = [-hop, hop]
        shifts, pieces = shifts + step, pieces + arrived
        if hop == 1:
            jobs = [Job(LEFT, grads_other, shifts, pieces)]
            jobs += [Job(j, features[j], shifts, pieces) for j in (LEFT, RIGHT)]
            other[LEFT], *own, grads_other = project(chips, split, jobs, True)
        else:
            jobs = [Job(LEFT, grads_other, step, arrived, other[LEFT])]
            jobs += [Job(j, features[j], step, arrived, own[j]) for j in (LEFT, RIGHT)]
            if hop + 1 == hops:
                jobs.append(Job(RIGHT, acts_other, step, arrived, other[RIGHT]))
            if hop + 1 < hops:
                other[LEFT], *own = project(chips, split, jobs)
            else:
                own = project(chips, split, jobs[1:3])
                other = project(chips, split, jobs[:1] + jobs[3:])
    upper, lower = moving
    upper, own, other = in_order(upper, own, other)
    last = [*upper, *lower]
    dense = finish(
        chips, hops, places, [*features, grads_other, acts_other], last, [*own, *other], norms,
        queries, rank,
    )
    factor = query_ids.shape[1] * math.sqrt(width * hidden / rank)
    return settle(lax.all_to_all(dense, AXIS, 0, 0), query_ids, seq_count, factor)


def on_device(*args):
    left_rows, right_rows = args[4].shape[0], args[5].shape[0]
    devices = lax.axis_size(AXIS)
    fits = (
        devices % 4 == 0
        and left_rows % 64 == 0
        and right_rows % 64 == 0
        and args[4].shape[1] % 256 == 0
        and args[6].shape[0] % 2 == 0
        and args[0].shape[1] % 128 == 0
        and (2 * left_rows) % 128 == 0
        and (2 * right_rows) % 128 == 0
    )
    return by_ring(*args) if fits else by_gathers(*args)


def solution(mesh):
    in_specs = (
        P(("groups", "dp"), None, None),
        P(("groups", "dp"), None, None),
        P(("groups", "dp"), None),
        P(("groups", "dp")),
        P("dp", "groups"),
        P("dp", "groups"),
        P("groups", None),
    )
    out_specs = P(("groups", "dp"), None)
    return jax.shard_map(
        on_device, mesh=mesh, in_specs=in_specs, out_specs=out_specs, check_vma=False
    )
```

```python
import functools
import math

import jax
import jax.numpy as jnp
from jax import lax
from jax.experimental import pallas as pl
from jax.experimental.pallas import tpu as pltpu
from jax.sharding import PartitionSpec as P

AXIS = "dp"
MIB = 1 << 20
ROWS = 256


def ring_order(chips):
    return list(range(0, chips, 2)) + list(range(chips - 1, 0, -2))


def xor_pairs(devices, mask):
    return [(i, i ^ mask) for i in range(devices)]


def ring_pairs(order, shift):
    chips = len(order)
    return [
        (order[k] * 2 + core, order[(k + shift) % chips] * 2 + core)
        for k in range(chips)
        for core in range(2)
    ]


def send(x, pairs):
    return lax.ppermute(x, AXIS, pairs)


def in_order(*values):
    return lax.optimization_barrier(values)


def device_index():
    return lax.axis_index(AXIS)


def chip_on_ring(chips, chip, shift):
    place = jnp.where(chip % 2 == 0, chip // 2, chips - 1 - chip // 2)
    place = (place + shift + chips) % chips
    return jnp.where(place < chips // 2, 2 * place, 2 * (chips - 1 - place) + 1)


SMEM = pl.BlockSpec(memory_space=pltpu.SMEM)
VMEM = pl.BlockSpec(memory_space=pltpu.VMEM)
ANY = pl.BlockSpec(memory_space=pl.ANY)
FLOAT = jnp.float32


def params(limit=60):
    return pltpu.CompilerParams(vmem_limit_bytes=limit * MIB)


def small_cost():
    return pl.CostEstimate(flops=1, bytes_accessed=1, transcendentals=0)


def dot(a, b):
    return jnp.dot(a, b, preferred_element_type=FLOAT)


def dot_rows(a, b, precision=None):
    return lax.dot_general(
        a, b, (((1,), (1,)), ((), ())), precision=precision, preferred_element_type=FLOAT
    )


def exact_dot(a, b):
    return jnp.dot(a, b, precision=lax.Precision.HIGHEST, preferred_element_type=FLOAT)


def split_kernel(left, right, mine, other):
    core = device_index() % 2
    low = left.shape[0]
    half = mine.shape[1]

    def put(target, first):
        target[0:low, :] = left[:, first : first + half]
        target[low:, :] = right[:, first : first + half]

    @pl.when(core == 0)
    def _():
        put(mine, 0)
        put(other, half)

    @pl.when(core != 0)
    def _():
        put(mine, half)
        put(other, 0)


def split_columns(left, right):
    rows, half = left.shape[0] + right.shape[0], left.shape[1] // 2
    return pl.pallas_call(
        split_kernel,
        in_specs=[VMEM, VMEM],
        out_specs=[VMEM, VMEM],
        out_shape=[jax.ShapeDtypeStruct((rows, half), left.dtype)] * 2,
        compiler_params=params(8),
        cost_estimate=small_cost(),
    )(left, right)


def merge_kernel(low, mine, came, upper, lower):
    core = device_index() % 2
    middle, total = upper.shape[0], upper.shape[0] + lower.shape[0]
    high = mine.shape[0] - low

    def put(first, second):
        parts = ((first, 0, low), (second, 0, low), (first, low, high), (second, low, high))
        at = 0
        for source, begin, count in parts:
            for target, start, stop in ((upper, 0, middle), (lower, middle, total)):
                lo, hi = max(at, start), min(at + count, stop)
                if lo < hi:
                    target[lo - start : hi - start, :] = source[begin + lo - at : begin + hi - at, :]
            at += count

    @pl.when(core == 0)
    def _():
        put(mine, came)

    @pl.when(core != 0)
    def _():
        put(came, mine)


def merge_rows(low, mine, came):
    return pl.pallas_call(
        functools.partial(merge_kernel, low),
        in_specs=[VMEM, VMEM],
        out_specs=[VMEM, VMEM],
        out_shape=[jax.ShapeDtypeStruct(mine.shape, mine.dtype)] * 2,
        compiler_params=params(8),
        cost_estimate=small_cost(),
    )(mine, came)


def block_of(chips, shift, features, rows=slice(None)):
    width = features.shape[1] // chips
    there = chip_on_ring(chips, device_index() // 2, shift)
    return features[rows, pl.ds(pl.multiple_of(there * width, 128), width)]


LEFT, RIGHT = 0, 1


class Job:
    def __init__(self, side, features, shifts, pieces, before=None):
        self.side, self.features, self.shifts, self.before = side, features, shifts, before
        self.pieces = pieces if side == RIGHT else pieces[::2]

    def operands(self):
        return [self.features, *self.pieces, *([] if self.before is None else [self.before])]


def project_kernel(jobs, split, chips, keep, *refs):
    rights = sum(len(job.shifts) for job in jobs if job.side == RIGHT)
    stacks, refs = (refs[-1], refs[:-1]) if rights else (None, refs)
    count = sum(len(job.operands()) for job in jobs)
    refs, outs = list(refs[:count]), list(refs[count:])
    work, used = [], 0
    for job in jobs:
        taken = [refs.pop(0) for _ in job.operands()]
        features, before = taken[0], None if job.before is None else taken.pop()
        factors = taken[1:]
        if job.side == RIGHT:
            for k in range(len(job.shifts)):
                upper, lower = factors[2 * k : 2 * k + 2]
                rest = upper.shape[0] - split
                stacks[used + k, 0:rest, :] = upper[split:, :]
                stacks[used + k, rest:, :] = lower[...]
            factors = [stacks.at[used + k] for k in range(len(job.shifts))]
            used += len(job.shifts)
        else:
            factors = [upper.at[0:split, :] for upper in factors]
        work.append((job, features, factors, before, outs.pop(0)))

    @pl.loop(0, work[0][1].shape[0] // ROWS)
    def _(i):
        rows = pl.ds(pl.multiple_of(i * ROWS, ROWS), ROWS)
        for job, features, factors, before, total in work:
            terms = [] if before is None else [before[rows, :]]
            for shift, factor in zip(job.shifts, factors):
                terms.append(dot(block_of(chips, shift, features, rows), factor[...]))
            total[rows, :] = sum(terms)
        if keep:
            outs[0][rows, :] = work[0][1][rows, :]


def project(chips, split, jobs, keep=False):
    first = jobs[0]
    tokens, columns = first.features.shape[0], first.pieces[0].shape[1]
    rights = [job for job in jobs if job.side == RIGHT]
    shapes = [jax.ShapeDtypeStruct((tokens, columns), FLOAT) for _ in jobs]
    if keep:
        shapes.append(jax.ShapeDtypeStruct(first.features.shape, first.features.dtype))
    aliases, place = {}, 0
    for k, job in enumerate(jobs):
        place += len(job.operands())
        if job.before is not None:
            aliases[place - 1] = k
    scratch = []
    if rights:
        total = sum(len(job.shifts) for job in rights)
        width = rights[0].features.shape[1] // chips
        scratch = [pltpu.VMEM((total, width, columns), first.features.dtype)]
    return pl.pallas_call(
        functools.partial(project_kernel, jobs, split, chips, keep),
        in_specs=[VMEM] * place,
        out_specs=[VMEM] * len(shapes),
        out_shape=shapes,
        scratch_shapes=scratch,
        input_output_aliases=aliases,
        compiler_params=params(14),
        cost_estimate=small_cost(),
    )(*[x for job in jobs for x in job.operands()])


def far_left_kernel(shift, chips, *refs):
    features, refs = refs[0:2], refs[2:]
    pieces, refs = refs[0:2], refs[2:]
    before, sums, stack = refs[0:2], refs[2:4], refs[4]
    first, split = pieces[0].shape[0], stack.shape[0]
    stack[0:first, :] = pieces[0][...]
    stack[first:, :] = pieces[1][0 : split - first, :]
    for x, old, new in zip(features, before, sums):
        new[...] = old[...] + dot(block_of(chips, shift, x), stack[...])


def far_left(chips, shift, features, pieces, sums):
    split, columns = features[0].shape[1] // chips, pieces[0].shape[1]
    return pl.pallas_call(
        functools.partial(far_left_kernel, shift, chips),
        in_specs=[VMEM] * 6,
        out_specs=[VMEM] * 2,
        out_shape=[jax.ShapeDtypeStruct(x.shape, x.dtype) for x in sums],
        scratch_shapes=[pltpu.VMEM((split, columns), pieces[0].dtype)],
        input_output_aliases={4: 0, 5: 1},
        compiler_params=params(8),
        cost_estimate=small_cost(),
    )(*features, *pieces, *sums)


def finish_kernel(
    shift, chips, rank, queries, skip, seq_index, seq_index_other, acts, acts_other, *refs
):
    pieces, refs = refs[:-8], refs[-8:]
    sums, sums_other = refs[0:2], refs[2:4]
    norms, dense, per_column, stack = refs[4:]
    columns = stack.shape[1]
    sequences = seq_index.shape[0]
    length = acts.shape[0] // sequences
    lanes = dense.shape[2] // sequences
    core = device_index() % 2
    column = lax.broadcasted_iota(jnp.int32, (columns, dense.shape[2]), 0)
    query = lax.broadcasted_iota(jnp.int32, (columns, dense.shape[2]), 1) % lanes
    member = (column // rank + core * (columns // rank) == query).astype(FLOAT)
    first = 0
    for piece in pieces:
        count = piece.shape[0] - skip
        stack[first : first + count, :] = piece[skip:, :]
        first, skip = first + count, 0
    sides = ((acts, sums), (acts_other, sums_other))
    for side, (features, total) in enumerate(sides):
        right = total[1][...] + dot(block_of(chips, shift, features), stack[...])
        product = total[0][...] * right
        for s in range(sequences):
            n = side * sequences + s
            per_column[n : n + 1, :] = jnp.sum(
                product[s * length : (s + 1) * length, :], axis=0, keepdims=True
            )
    raw = exact_dot(per_column[...], member)
    lane = lax.broadcasted_iota(jnp.int32, dense.shape, 2)
    slot = lax.broadcasted_iota(jnp.int32, dense.shape, 0) * sequences + lane // lanes
    last = lane[0] % lanes == queries
    placed = jnp.zeros(dense.shape, FLOAT)
    for side, places in enumerate((seq_index, seq_index_other)):
        for s in range(sequences):
            n = side * sequences + s
            row = raw[n : n + 1, :]
            if side == 0:
                row = row + jnp.where(last, norms[s, 0:1, 0:1], 0.0)
            placed = placed + jnp.where(slot == places[s], row[None], 0.0)
    dense[...] = placed


def settle_kernel(factor, parts, query_ids, influence):
    sequences, queries = influence.shape
    lanes = parts.shape[2] // sequences
    total = jnp.sum(parts[...], axis=0)
    asked = (query_ids[...] != 0).astype(FLOAT)
    count = dot_rows(jnp.ones((8, asked.shape[1]), FLOAT), asked, lax.Precision.HIGHEST)[0:1, :]
    for s in range(sequences):
        at = s * lanes
        norm = jnp.sqrt(total[:, at + queries : at + queries + 1] + 1e-06)
        influence[s : s + 1, :] = total[:, at : at + queries] * factor / (count * norm)


def settle(parts, query_ids, sequences, factor):
    return pl.pallas_call(
        functools.partial(settle_kernel, factor),
        in_specs=[VMEM, VMEM],
        out_specs=VMEM,
        out_shape=jax.ShapeDtypeStruct((sequences, query_ids.shape[0]), FLOAT),
        compiler_params=params(4),
        cost_estimate=small_cost(),
    )(parts, query_ids)


def finish(chips, shift, places, features, pieces, skip, sums, norms, queries, rank):
    columns = pieces[0].shape[1]
    lanes = -(-places[0].shape[0] * (queries + 1) // 128) * 128
    return pl.pallas_call(
        functools.partial(finish_kernel, shift, chips, rank, queries, skip),
        in_specs=[SMEM] * 2 + [VMEM] * (7 + len(pieces)),
        out_specs=VMEM,
        out_shape=jax.ShapeDtypeStruct((2 * chips, 1, lanes), FLOAT),
        scratch_shapes=[
            pltpu.VMEM((2 * places[0].shape[0], columns), FLOAT),
            pltpu.VMEM((features[0].shape[1] // chips, columns), pieces[0].dtype),
        ],
        compiler_params=params(12),
        cost_estimate=small_cost(),
    )(*places, *features, *pieces, *sums, norms)


def norms_kernel(sequences, grads, acts, norms):
    length = grads.shape[0] // sequences
    for s in range(sequences):
        rows = slice(s * length, (s + 1) * length)
        value = dot_rows(grads[rows, :], grads[rows, :]) * dot_rows(acts[rows, :], acts[rows, :])
        norms[s] = jnp.broadcast_to(jnp.sum(value, keepdims=True), norms.shape[1:])


def squared_norms_of(sequences, grads, acts):
    return pl.pallas_call(
        functools.partial(norms_kernel, sequences),
        in_specs=[VMEM, VMEM],
        out_specs=VMEM,
        out_shape=jax.ShapeDtypeStruct((sequences, 8, 128), FLOAT),
        compiler_params=params(8),
        cost_estimate=small_cost(),
    )(grads, acts)


def squared_norms(live, grads, acts):
    def covariance(x):
        return jnp.einsum("hcp,hqp->hcq", x, x, preferred_element_type=jnp.float32)

    return jnp.sum(
        live[:, :, None] * live[:, None, :] * covariance(grads) * covariance(acts), axis=(1, 2)
    )


def to_owners(dense, seq_count, mask=1):
    devices = lax.axis_size(AXIS)
    if devices & (devices - 1):
        return lax.psum_scatter(dense, AXIS, scatter_dimension=0, tiled=True)
    while mask < devices:
        masks = [mask] if mask < 4 or 2 * mask >= devices else [3 * mask, 2 * mask, mask]
        dense = sum([send(dense, xor_pairs(devices, m)) for m in masks], dense)
        mask *= len(masks) + 1
    return lax.dynamic_slice_in_dim(dense, lax.axis_index(AXIS) * seq_count, seq_count, axis=0)


def by_gathers(
    training_output_gradients, training_activations, train_ids, seq_index,
    left_factor, input_side_factor, query_ids,
):
    seq_count, length, width = training_output_gradients.shape
    hidden = training_activations.shape[2]
    columns = left_factor.shape[1]
    queries = query_ids.shape[0]
    rank = columns // queries
    grads = training_output_gradients.reshape(seq_count * length, width)
    acts = training_activations.reshape(seq_count * length, hidden)
    proj_out = dot(grads, lax.all_gather(left_factor, AXIS, axis=0, tiled=True))
    proj_in = dot(acts, lax.all_gather(input_side_factor, AXIS, axis=0, tiled=True))
    live = (train_ids != 0).astype(jnp.float32)
    product = (proj_out * proj_in).reshape(seq_count, length, columns) * live[:, :, None]
    raw = jnp.sum(jnp.sum(product, axis=1).reshape(seq_count, queries, rank), axis=2)
    grad_sq = squared_norms(live, training_output_gradients, training_activations)
    count = jnp.sum((query_ids != 0).astype(jnp.float32), axis=1)
    factor = query_ids.shape[1] * math.sqrt(width * hidden / rank)
    score = raw * factor / (count[None, :] * jnp.sqrt(grad_sq + 1e-06)[:, None])
    slots = jnp.arange(seq_count * lax.axis_size(AXIS), dtype=jnp.int32)
    dense = jnp.sum(
        jnp.where(seq_index[:, None, None] == slots[None, :, None], score[:, None, :], 0.0), axis=0
    )
    return to_owners(dense, seq_count)


def by_ring(
    training_output_gradients, training_activations, train_ids, seq_index,
    left_factor, input_side_factor, query_ids,
):
    seq_count, length, width = training_output_gradients.shape
    hidden = training_activations.shape[2]
    columns = left_factor.shape[1]
    queries = query_ids.shape[0]
    rank = columns // queries
    devices = lax.axis_size(AXIS)
    chips = devices // 2
    hops = chips // 2
    swap = xor_pairs(devices, 1)
    order = ring_order(chips)
    forward, backward = ring_pairs(order, 1), ring_pairs(order, -1)
    grads = training_output_gradients.reshape(seq_count * length, width)
    acts = training_activations.reshape(seq_count * length, hidden)
    low = left_factor.shape[0]

    mine, other = split_columns(left_factor, input_side_factor)
    came = send(other, swap)
    places = [seq_index, send(seq_index, swap)]
    pieces = list(merge_rows(low, mine, came))
    pieces, places, grads_sent, train_ids = in_order(pieces, places, grads, train_ids)
    moving = [[send(x, forward), send(x, backward)] for x in pieces]
    acts = jnp.where((train_ids != 0).reshape(-1, 1), acts, jnp.zeros_like(acts))
    features = [grads, acts]
    grads_other = send(grads_sent, swap)
    norms = squared_norms_of(seq_count, grads, acts)
    middle = pieces[0].shape[0] // 2
    split = width // chips
    shifts = [0]
    own = [None, None]
    other = [None, None]
    for hop in range(1, hops):
        if hop == 1:
            moving, norms, places, acts_sent, grads_other = in_order(
                moving, norms, places, acts, grads_other
            )
            acts_other = send(acts_sent, swap)
            new = moving
        else:
            upper, own, other[LEFT] = in_order(moving[0], own, other[LEFT])
            lower = moving[1]
            if hop + 1 == hops:
                (other[RIGHT],) = project(
                    chips, split, [Job(RIGHT, acts_other, shifts, pieces)]
                )
                *lower, other[RIGHT] = in_order(*lower, other[RIGHT])
            new = [upper, lower]
        arrived = [new[0][0], new[1][0], new[0][1], new[1][1]]
        if hop + 1 == hops:
            new = [[x[0][:middle], x[1][middle:]] for x in new]
        moving = [[send(x[0], forward), send(x[1], backward)] for x in new]
        step = [-hop, hop]
        shifts, pieces = shifts + step, pieces + arrived
        if hop == 1:
            jobs = [Job(LEFT, grads_other, shifts, pieces)]
            jobs += [Job(j, features[j], shifts, pieces) for j in (LEFT, RIGHT)]
            other[LEFT], *own, grads_other = project(chips, split, jobs, True)
        else:
            jobs = [Job(LEFT, grads_other, step, arrived, other[LEFT])]
            jobs += [Job(j, features[j], step, arrived, own[j]) for j in (LEFT, RIGHT)]
            if hop + 1 == hops:
                jobs.append(Job(RIGHT, acts_other, step, arrived, other[RIGHT]))
            if hop + 1 < hops:
                other[LEFT], *own = project(chips, split, jobs)
            else:
                own = project(chips, split, jobs[1:3])
                other = project(chips, split, jobs[:1] + jobs[3:])
    upper, lower = moving
    upper, own, other = in_order(upper, own, other)
    own, other = list(own), list(other)
    own[LEFT], other[LEFT] = far_left(
        chips, hops, [grads, grads_other], upper, [own[LEFT], other[LEFT]]
    )
    dense = finish(
        chips, hops, places, [acts, acts_other], [upper[1], *lower], split - middle,
        [*own, *other], norms, queries, rank,
    )
    factor = query_ids.shape[1] * math.sqrt(width * hidden / rank)
    return settle(lax.all_to_all(dense, AXIS, 0, 0), query_ids, seq_count, factor)


def on_device(*args):
    left_rows, right_rows = args[4].shape[0], args[5].shape[0]
    devices = lax.axis_size(AXIS)
    fits = (
        devices % 4 == 0
        and devices >= 12
        and left_rows + right_rows <= 4 * left_rows <= 2 * (left_rows + right_rows)
        and left_rows % 64 == 0
        and right_rows % 64 == 0
        and args[4].shape[1] % 256 == 0
        and args[6].shape[0] % 2 == 0
        and args[0].shape[1] % 128 == 0
        and (2 * left_rows) % 128 == 0
        and (2 * right_rows) % 128 == 0
    )
    return by_ring(*args) if fits else by_gathers(*args)


def solution(mesh):
    in_specs = (
        P(("groups", "dp"), None, None),
        P(("groups", "dp"), None, None),
        P(("groups", "dp"), None),
        P(("groups", "dp")),
        P("dp", "groups"),
        P("dp", "groups"),
        P("groups", None),
    )
    out_specs = P(("groups", "dp"), None)
    return jax.shard_map(
        on_device, mesh=mesh, in_specs=in_specs, out_specs=out_specs, check_vma=False
    )
```

```python
import functools
import math

import jax
import jax.numpy as jnp
from jax import lax
from jax.experimental import pallas as pl
from jax.experimental.pallas import tpu as pltpu
from jax.sharding import PartitionSpec as P

AXIS = "dp"
MIB = 1 << 20
ROWS = 256


def ring_order(chips):
    return list(range(0, chips, 2)) + list(range(chips - 1, 0, -2))


def xor_pairs(devices, mask):
    return [(i, i ^ mask) for i in range(devices)]


def ring_pairs(order, shift):
    chips = len(order)
    return [
        (order[k] * 2 + core, order[(k + shift) % chips] * 2 + core)
        for k in range(chips)
        for core in range(2)
    ]


def send(x, pairs):
    return lax.ppermute(x, AXIS, pairs)


def in_order(*values):
    return lax.optimization_barrier(values)


def device_index():
    return lax.axis_index(AXIS)


def chip_on_ring(chips, chip, shift):
    place = jnp.where(chip % 2 == 0, chip // 2, chips - 1 - chip // 2)
    place = (place + shift + chips) % chips
    return jnp.where(place < chips // 2, 2 * place, 2 * (chips - 1 - place) + 1)


SMEM = pl.BlockSpec(memory_space=pltpu.SMEM)
VMEM = pl.BlockSpec(memory_space=pltpu.VMEM)
ANY = pl.BlockSpec(memory_space=pl.ANY)
FLOAT = jnp.float32


def params(limit=60):
    return pltpu.CompilerParams(vmem_limit_bytes=limit * MIB)


def small_cost():
    return pl.CostEstimate(flops=1, bytes_accessed=1, transcendentals=0)


def dot(a, b):
    return jnp.dot(a, b, preferred_element_type=FLOAT)


def dot_rows(a, b, precision=None):
    return lax.dot_general(
        a, b, (((1,), (1,)), ((), ())), precision=precision, preferred_element_type=FLOAT
    )


def exact_dot(a, b):
    return jnp.dot(a, b, precision=lax.Precision.HIGHEST, preferred_element_type=FLOAT)


def split_kernel(left, right, mine, other):
    core = device_index() % 2
    low = left.shape[0]
    half = mine.shape[1]

    def put(target, first):
        target[0:low, :] = left[:, first : first + half]
        target[low:, :] = right[:, first : first + half]

    @pl.when(core == 0)
    def _():
        put(mine, 0)
        put(other, half)

    @pl.when(core != 0)
    def _():
        put(mine, half)
        put(other, 0)


def split_columns(left, right):
    rows, half = left.shape[0] + right.shape[0], left.shape[1] // 2
    return pl.pallas_call(
        split_kernel,
        in_specs=[VMEM, VMEM],
        out_specs=[VMEM, VMEM],
        out_shape=[jax.ShapeDtypeStruct((rows, half), left.dtype)] * 2,
        compiler_params=params(8),
        cost_estimate=small_cost(),
    )(left, right)


def merge_kernel(low, mine, came, upper, lower):
    core = device_index() % 2
    middle, total = upper.shape[0], upper.shape[0] + lower.shape[0]
    high = mine.shape[0] - low

    def put(first, second):
        parts = ((first, 0, low), (second, 0, low), (first, low, high), (second, low, high))
        at = 0
        for source, begin, count in parts:
            for target, start, stop in ((upper, 0, middle), (lower, middle, total)):
                lo, hi = max(at, start), min(at + count, stop)
                if lo < hi:
                    target[lo - start : hi - start, :] = source[begin + lo - at : begin + hi - at, :]
            at += count

    @pl.when(core == 0)
    def _():
        put(mine, came)

    @pl.when(core != 0)
    def _():
        put(came, mine)


def merge_rows(low, mine, came):
    return pl.pallas_call(
        functools.partial(merge_kernel, low),
        in_specs=[VMEM, VMEM],
        out_specs=[VMEM, VMEM],
        out_shape=[jax.ShapeDtypeStruct(mine.shape, mine.dtype)] * 2,
        compiler_params=params(8),
        cost_estimate=small_cost(),
    )(mine, came)


def block_of(chips, shift, features, rows=slice(None)):
    width = features.shape[1] // chips
    there = chip_on_ring(chips, device_index() // 2, shift)
    return features[rows, pl.ds(pl.multiple_of(there * width, 128), width)]


LEFT, RIGHT = 0, 1


class Job:
    def __init__(self, side, features, shifts, pieces, before=None):
        self.side, self.features, self.shifts, self.before = side, features, shifts, before
        self.pieces = pieces if side == RIGHT else pieces[::2]

    def operands(self):
        return [self.features, *self.pieces, *([] if self.before is None else [self.before])]


def project_kernel(jobs, split, chips, keep, *refs):
    rights = sum(len(job.shifts) for job in jobs if job.side == RIGHT)
    stacks, refs = (refs[-1], refs[:-1]) if rights else (None, refs)
    count = sum(len(job.operands()) for job in jobs)
    refs, outs = list(refs[:count]), list(refs[count:])
    work, used = [], 0
    for job in jobs:
        taken = [refs.pop(0) for _ in job.operands()]
        features, before = taken[0], None if job.before is None else taken.pop()
        factors = taken[1:]
        if job.side == RIGHT:
            for k in range(len(job.shifts)):
                upper, lower = factors[2 * k : 2 * k + 2]
                rest = upper.shape[0] - split
                stacks[used + k, 0:rest, :] = upper[split:, :]
                stacks[used + k, rest:, :] = lower[...]
            factors = [stacks.at[used + k] for k in range(len(job.shifts))]
            used += len(job.shifts)
        else:
            factors = [upper.at[0:split, :] for upper in factors]
        work.append((job, features, factors, before, outs.pop(0)))

    @pl.loop(0, work[0][1].shape[0] // ROWS)
    def _(i):
        rows = pl.ds(pl.multiple_of(i * ROWS, ROWS), ROWS)
        for job, features, factors, before, total in work:
            terms = [] if before is None else [before[rows, :]]
            for shift, factor in zip(job.shifts, factors):
                terms.append(dot(block_of(chips, shift, features, rows), factor[...]))
            total[rows, :] = sum(terms)
        if keep:
            outs[0][rows, :] = work[0][1][rows, :]


def project(chips, split, jobs, keep=False):
    first = jobs[0]
    tokens, columns = first.features.shape[0], first.pieces[0].shape[1]
    rights = [job for job in jobs if job.side == RIGHT]
    shapes = [jax.ShapeDtypeStruct((tokens, columns), FLOAT) for _ in jobs]
    if keep:
        shapes.append(jax.ShapeDtypeStruct(first.features.shape, first.features.dtype))
    aliases, place = {}, 0
    for k, job in enumerate(jobs):
        place += len(job.operands())
        if job.before is not None:
            aliases[place - 1] = k
    scratch = []
    if rights:
        total = sum(len(job.shifts) for job in rights)
        width = rights[0].features.shape[1] // chips
        scratch = [pltpu.VMEM((total, width, columns), first.features.dtype)]
    return pl.pallas_call(
        functools.partial(project_kernel, jobs, split, chips, keep),
        in_specs=[VMEM] * place,
        out_specs=[VMEM] * len(shapes),
        out_shape=shapes,
        scratch_shapes=scratch,
        input_output_aliases=aliases,
        compiler_params=params(14),
        cost_estimate=small_cost(),
    )(*[x for job in jobs for x in job.operands()])


def far_left_kernel(shift, chips, *refs):
    features, refs = refs[0:2], refs[2:]
    pieces, refs = refs[0:2], refs[2:]
    before, sums, stack = refs[0:2], refs[2:4], refs[4]
    first, split = pieces[0].shape[0], stack.shape[0]
    stack[0:first, :] = pieces[0][...]
    stack[first:, :] = pieces[1][0 : split - first, :]
    for x, old, new in zip(features, before, sums):
        new[...] = old[...] + dot(block_of(chips, shift, x), stack[...])


def far_left(chips, shift, features, pieces, sums):
    split, columns = features[0].shape[1] // chips, pieces[0].shape[1]
    return pl.pallas_call(
        functools.partial(far_left_kernel, shift, chips),
        in_specs=[VMEM] * 6,
        out_specs=[VMEM] * 2,
        out_shape=[jax.ShapeDtypeStruct(x.shape, x.dtype) for x in sums],
        scratch_shapes=[pltpu.VMEM((split, columns), pieces[0].dtype)],
        input_output_aliases={4: 0, 5: 1},
        compiler_params=params(8),
        cost_estimate=small_cost(),
    )(*features, *pieces, *sums)


def finish_kernel(
    shift, chips, rank, queries, skip, seq_index, seq_index_other, acts, acts_other, *refs
):
    pieces, refs = refs[:-8], refs[-8:]
    sums, sums_other = refs[0:2], refs[2:4]
    norms, dense, per_column, stack = refs[4:]
    columns = stack.shape[1]
    sequences = seq_index.shape[0]
    length = acts.shape[0] // sequences
    lanes = dense.shape[2] // sequences
    core = device_index() % 2
    column = lax.broadcasted_iota(jnp.int32, (columns, dense.shape[2]), 0)
    query = lax.broadcasted_iota(jnp.int32, (columns, dense.shape[2]), 1) % lanes
    begin = (query - core * (columns // rank)) * rank
    member = ((column >= begin) & (column < begin + rank)).astype(FLOAT)
    first = 0
    for piece in pieces:
        count = piece.shape[0] - skip
        stack[first : first + count, :] = piece[skip:, :]
        first, skip = first + count, 0
    sides = ((acts, sums), (acts_other, sums_other))
    for side, (features, total) in enumerate(sides):
        right = total[1][...] + dot(block_of(chips, shift, features), stack[...])
        product = total[0][...] * right
        for s in range(sequences):
            n = side * sequences + s
            per_column[n : n + 1, :] = jnp.sum(
                product[s * length : (s + 1) * length, :], axis=0, keepdims=True
            )
    raw = exact_dot(per_column[...], member)
    lane = lax.broadcasted_iota(jnp.int32, dense.shape, 2)
    slot = lax.broadcasted_iota(jnp.int32, dense.shape, 0) * sequences + lane // lanes
    last = lane[0] % lanes == queries
    placed = jnp.zeros(dense.shape, FLOAT)
    for side, places in enumerate((seq_index, seq_index_other)):
        for s in range(sequences):
            n = side * sequences + s
            row = raw[n : n + 1, :]
            if side == 0:
                row = row + jnp.where(last, norms[s, 0:1, 0:1], 0.0)
            placed = placed + jnp.where(slot == places[s], row[None], 0.0)
    dense[...] = placed


def settle_kernel(parts, norms, influence):
    sequences, queries = influence.shape
    lanes = parts.shape[2] // sequences
    total = jnp.sum(parts[...], axis=0)
    weight = norms[sequences, 0:1, 0:queries]
    for s in range(sequences):
        at = s * lanes
        norm = jnp.sqrt(total[:, at + queries : at + queries + 1] + 1e-06)
        influence[s : s + 1, :] = total[:, at : at + queries] * weight / norm


def settle(parts, norms, sequences, queries):
    return pl.pallas_call(
        settle_kernel,
        in_specs=[VMEM, VMEM],
        out_specs=VMEM,
        out_shape=jax.ShapeDtypeStruct((sequences, queries), FLOAT),
        compiler_params=params(4),
        cost_estimate=small_cost(),
    )(parts, norms)


def finish(chips, shift, places, features, pieces, skip, sums, norms, queries, rank):
    columns = pieces[0].shape[1]
    lanes = -(-places[0].shape[0] * (queries + 1) // 128) * 128
    return pl.pallas_call(
        functools.partial(finish_kernel, shift, chips, rank, queries, skip),
        in_specs=[SMEM] * 2 + [VMEM] * (7 + len(pieces)),
        out_specs=VMEM,
        out_shape=jax.ShapeDtypeStruct((2 * chips, 1, lanes), FLOAT),
        scratch_shapes=[
            pltpu.VMEM((2 * places[0].shape[0], columns), FLOAT),
            pltpu.VMEM((features[0].shape[1] // chips, columns), pieces[0].dtype),
        ],
        compiler_params=params(12),
        cost_estimate=small_cost(),
    )(*places, *features, *pieces, *sums, norms)


def norms_kernel(sequences, factor, grads, acts, query_ids, norms):
    length = grads.shape[0] // sequences
    for s in range(sequences):
        rows = slice(s * length, (s + 1) * length)
        value = dot_rows(grads[rows, :], grads[rows, :]) * dot_rows(acts[rows, :], acts[rows, :])
        norms[s] = jnp.broadcast_to(jnp.sum(value, keepdims=True), norms.shape[1:])
    asked = (query_ids[...] != 0).astype(FLOAT)
    count = dot_rows(jnp.ones((8, asked.shape[1]), FLOAT), asked, lax.Precision.HIGHEST)
    norms[sequences, :, 0 : asked.shape[0]] = factor / count


def squared_norms_of(sequences, factor, grads, acts, query_ids):
    return pl.pallas_call(
        functools.partial(norms_kernel, sequences, factor),
        in_specs=[VMEM] * 3,
        out_specs=VMEM,
        out_shape=jax.ShapeDtypeStruct((sequences + 1, 8, 128), FLOAT),
        compiler_params=params(8),
        cost_estimate=small_cost(),
    )(grads, acts, query_ids)


def squared_norms(live, grads, acts):
    def covariance(x):
        return jnp.einsum("hcp,hqp->hcq", x, x, preferred_element_type=jnp.float32)

    return jnp.sum(
        live[:, :, None] * live[:, None, :] * covariance(grads) * covariance(acts), axis=(1, 2)
    )


def to_owners(dense, seq_count, mask=1):
    devices = lax.axis_size(AXIS)
    if devices & (devices - 1):
        return lax.psum_scatter(dense, AXIS, scatter_dimension=0, tiled=True)
    while mask < devices:
        masks = [mask] if mask < 4 or 2 * mask >= devices else [3 * mask, 2 * mask, mask]
        dense = sum([send(dense, xor_pairs(devices, m)) for m in masks], dense)
        mask *= len(masks) + 1
    return lax.dynamic_slice_in_dim(dense, lax.axis_index(AXIS) * seq_count, seq_count, axis=0)


def by_gathers(
    training_output_gradients, training_activations, train_ids, seq_index,
    left_factor, input_side_factor, query_ids,
):
    seq_count, length, width = training_output_gradients.shape
    hidden = training_activations.shape[2]
    columns = left_factor.shape[1]
    queries = query_ids.shape[0]
    rank = columns // queries
    grads = training_output_gradients.reshape(seq_count * length, width)
    acts = training_activations.reshape(seq_count * length, hidden)
    proj_out = dot(grads, lax.all_gather(left_factor, AXIS, axis=0, tiled=True))
    proj_in = dot(acts, lax.all_gather(input_side_factor, AXIS, axis=0, tiled=True))
    live = (train_ids != 0).astype(jnp.float32)
    product = (proj_out * proj_in).reshape(seq_count, length, columns) * live[:, :, None]
    raw = jnp.sum(jnp.sum(product, axis=1).reshape(seq_count, queries, rank), axis=2)
    grad_sq = squared_norms(live, training_output_gradients, training_activations)
    count = jnp.sum((query_ids != 0).astype(jnp.float32), axis=1)
    factor = query_ids.shape[1] * math.sqrt(width * hidden / rank)
    score = raw * factor / (count[None, :] * jnp.sqrt(grad_sq + 1e-06)[:, None])
    slots = jnp.arange(seq_count * lax.axis_size(AXIS), dtype=jnp.int32)
    dense = jnp.sum(
        jnp.where(seq_index[:, None, None] == slots[None, :, None], score[:, None, :], 0.0), axis=0
    )
    return to_owners(dense, seq_count)


def by_ring(
    training_output_gradients, training_activations, train_ids, seq_index,
    left_factor, input_side_factor, query_ids,
):
    seq_count, length, width = training_output_gradients.shape
    hidden = training_activations.shape[2]
    columns = left_factor.shape[1]
    queries = query_ids.shape[0]
    rank = columns // queries
    devices = lax.axis_size(AXIS)
    chips = devices // 2
    hops = chips // 2
    swap = xor_pairs(devices, 1)
    order = ring_order(chips)
    forward, backward = ring_pairs(order, 1), ring_pairs(order, -1)
    grads = training_output_gradients.reshape(seq_count * length, width)
    acts = training_activations.reshape(seq_count * length, hidden)
    low = left_factor.shape[0]

    mine, other = split_columns(left_factor, input_side_factor)
    came = send(other, swap)
    places = [seq_index, send(seq_index, swap)]
    pieces = list(merge_rows(low, mine, came))
    pieces, places, grads_sent, train_ids = in_order(pieces, places, grads, train_ids)
    moving = [[send(x, forward), send(x, backward)] for x in pieces]
    acts = jnp.where((train_ids != 0).reshape(-1, 1), acts, jnp.zeros_like(acts))
    features = [grads, acts]
    grads_other = send(grads_sent, swap)
    factor = query_ids.shape[1] * math.sqrt(width * hidden / rank)
    norms = squared_norms_of(seq_count, factor, grads, acts, query_ids)
    middle = pieces[0].shape[0] // 2
    split = width // chips
    shifts = [0]
    own = [None, None]
    other = [None, None]
    for hop in range(1, hops):
        if hop == 1:
            moving, norms, places, acts_sent, grads_other = in_order(
                moving, norms, places, acts, grads_other
            )
            acts_other = send(acts_sent, swap)
            new = moving
        else:
            upper, own, other[LEFT] = in_order(moving[0], own, other[LEFT])
            lower = moving[1]
            if hop + 1 == hops:
                (other[RIGHT],) = project(
                    chips, split, [Job(RIGHT, acts_other, shifts, pieces)]
                )
                *lower, other[RIGHT] = in_order(*lower, other[RIGHT])
            new = [upper, lower]
        arrived = [new[0][0], new[1][0], new[0][1], new[1][1]]
        if hop + 1 == hops:
            new = [[x[0][:middle], x[1][middle:]] for x in new]
        moving = [[send(x[0], forward), send(x[1], backward)] for x in new]
        step = [-hop, hop]
        shifts, pieces = shifts + step, pieces + arrived
        if hop == 1:
            jobs = [Job(LEFT, grads_other, shifts, pieces)]
            jobs += [Job(j, features[j], shifts, pieces) for j in (LEFT, RIGHT)]
            other[LEFT], *own, grads_other = project(chips, split, jobs, True)
        else:
            jobs = [Job(LEFT, grads_other, step, arrived, other[LEFT])]
            jobs += [Job(j, features[j], step, arrived, own[j]) for j in (LEFT, RIGHT)]
            if hop + 1 == hops:
                jobs.append(Job(RIGHT, acts_other, step, arrived, other[RIGHT]))
            if hop + 1 < hops:
                other[LEFT], *own = project(chips, split, jobs)
            else:
                own = project(chips, split, jobs[1:3])
                other = project(chips, split, jobs[:1] + jobs[3:])
    upper, lower = moving
    upper, own, other = in_order(upper, own, other)
    own, other = list(own), list(other)
    own[LEFT], other[LEFT] = far_left(
        chips, hops, [grads, grads_other], upper, [own[LEFT], other[LEFT]]
    )
    dense = finish(
        chips, hops, places, [acts, acts_other], [upper[1], *lower], split - middle,
        [*own, *other], norms, queries, rank,
    )
    return settle(lax.all_to_all(dense, AXIS, 0, 0), norms, seq_count, queries)


def on_device(*args):
    left_rows, right_rows = args[4].shape[0], args[5].shape[0]
    devices = lax.axis_size(AXIS)
    fits = (
        devices % 4 == 0
        and devices >= 12
        and left_rows + right_rows <= 4 * left_rows <= 2 * (left_rows + right_rows)
        and left_rows % 64 == 0
        and right_rows % 64 == 0
        and args[4].shape[1] % 256 == 0
        and args[6].shape[0] % 2 == 0
        and args[0].shape[1] % 128 == 0
        and (2 * left_rows) % 128 == 0
        and (2 * right_rows) % 128 == 0
    )
    return by_ring(*args) if fits else by_gathers(*args)


def solution(mesh):
    in_specs = (
        P(("groups", "dp"), None, None),
        P(("groups", "dp"), None, None),
        P(("groups", "dp"), None),
        P(("groups", "dp")),
        P("dp", "groups"),
        P("dp", "groups"),
        P("groups", None),
    )
    out_specs = P(("groups", "dp"), None)
    return jax.shard_map(
        on_device, mesh=mesh, in_specs=in_specs, out_specs=out_specs, check_vma=False
    )
```
